256 devices in a mesh: region: 32 (over x, z), sub: 8 (over y, core).
Axes of the slice: x: 4, y: 4, z: 8, core: 2. Of those that a mesh axis runs over, the one named last changes fastest.
Arguments:
- directions: float32 [2, 64, 256, 2048], P(None, None, 'region', 'sub'), may hold values from -6 to 6
- diag_blocks: float32 [4, 4, 256, 2048], P(None, None, 'region', 'sub'), may hold values from -2 to 2
- left_blocks: float32 [4, 4, 256, 2048], P(None, None, 'region', 'sub'), may hold values from -1.5 to 1.5
- right_blocks: float32 [4, 4, 256, 2048], P(None, None, 'region', 'sub'), may hold values from -1.5 to 1.5
- param_blocks: float32 [4, 2, 256, 2048], P(None, None, 'region', 'sub'), may hold values from -6 to 6
- obs_weight: float32 [4, 256, 2048], P(None, 'region', 'sub'), may hold values from 0.3 to 3
- end_junction: int32 [2, 256, 1], replicated, may hold values from 0 to 255
Outputs:
- hess_dirs: float32 [2, 64, 256, 2048], P(None, None, 'region', 'sub')
The draws below stay inside these ranges and needn't reach their ends.
Inputs may be any that keep to these rules, and one draw needn't show every extreme that they name: `end_junction`: every junction is named by at least one pipe end.
All inputs are finite; a program needn't handle non-finite values.
Results may differ from the reference program's by a relative error of at most 0.0001.
Values sent between devices are 32-bit elements; how exact they have to be, the bound alone decides.
A program may use at most 128 MiB of HBM per device.

```python
import math
import jax
import jax.numpy as jnp
from jax import lax

COMP = 4
NPAR = 2
R = 64
STEPS = 2
NPIPES = 256
PIPE_LEN = 2048
NJ = 256


def shard_levels(stream_key, shape, split, low, largest):
    def one(axis_at, blocks):
        heights = jax.random.uniform(jax.random.fold_in(jax.random.fold_in(stream_key, 6), axis_at), (blocks,), jnp.float32, low / len(split), largest / len(split))
        return jnp.repeat(jnp.exp(heights), shape[axis_at] // blocks).reshape((-1,) + (1,) * (len(shape) - axis_at - 1))

    gain = one(*split[0])
    for cut in split[1:]:
        gain = gain * one(*cut)
    return gain


def distinct(rng, rows, count, top, lift):
    ranking = jax.random.permutation(jax.random.fold_in(rng, 1), count)
    pull = ranking
    for power in range(3):
        pull = pull * pull // count
    pull = pull * lift // count
    chance = jax.random.randint(jax.random.fold_in(rng, 2), (rows, count), 0, 4096) + pull
    holders = jax.random.permutation(jax.random.fold_in(rng, 3), rows)[jnp.arange(count) % rows]
    chance = jnp.where(jnp.arange(rows)[:, None] == holders[None, :], 1 << 14, chance)
    score = chance * count + jnp.arange(count)
    return lax.top_k(score.astype(jnp.int32), top)[1].astype(jnp.int32)


def noise(own_key, extent, width, bound, cuts=(), kind=jnp.bfloat16):
    entries = jax.random.normal(own_key, extent, jnp.float32) * width
    if len(cuts) > 0:
        entries = shard_levels(own_key, extent, cuts, -0.22, 0.18) * entries
    return jnp.clip(entries, min=-bound, max=bound).astype(kind)


def setup_inputs(seed: int = 0) -> dict:
    arg_keys = jax.random.split(jax.random.key(seed), 8)
    return {
        "directions": noise(arg_keys[0], (NPAR, R, NPIPES, PIPE_LEN), 1.0, 6.0, ((2, 32), (3, 8)), jnp.float32),
        "diag_blocks": noise(arg_keys[1], (COMP, COMP, NPIPES, PIPE_LEN), 0.15, 2.0, ((2, 32), (3, 8)), jnp.float32),
        "left_blocks": noise(arg_keys[2], (COMP, COMP, NPIPES, PIPE_LEN), 0.1, 1.5, ((2, 32), (3, 8)), jnp.float32),
        "right_blocks": noise(arg_keys[3], (COMP, COMP, NPIPES, PIPE_LEN), 0.1, 1.5, ((2, 32), (3, 8)), jnp.float32),
        "param_blocks": noise(arg_keys[4], (COMP, NPAR, NPIPES, PIPE_LEN), 0.5, 6.0, ((2, 32), (3, 8)), jnp.float32),
        "obs_weight": jnp.clip(jnp.exp(math.log(3.0) - 2.3025851 * jax.random.uniform(arg_keys[5], (COMP, NPIPES, PIPE_LEN), jnp.float32) ** shard_levels(arg_keys[5], (COMP, NPIPES, PIPE_LEN), ((1, 32), (2, 8)), -0.2, 0.2)), 0.3, 3.0),
        "end_junction": distinct(arg_keys[6], 2 * NPIPES, NJ, 1, 64).reshape((2, NPIPES, 1)),
    }


junction_rate = 0.5
column_group = 8


def block_apply(blocks, state_in, flipped):
    out_count = blocks.shape[1] if flipped else blocks.shape[0]
    summed = jnp.zeros((out_count,) + state_in.shape[1:], jnp.float32)
    for member in range(state_in.shape[0]):
        factor = blocks[member] if flipped else blocks[:, member]
        summed = summed + factor[:, None] * state_in[member][None]
    return summed


def junction_add(state_in, junction_ids, degree):
    components, columns, pipe_count = state_in.shape[0], state_in.shape[1], state_in.shape[2]
    edge_vals = jnp.stack([state_in[..., 0], state_in[..., -1]], axis=0)
    end_states = jnp.transpose(edge_vals, (0, 3, 1, 2)).reshape(2 * pipe_count, components, columns)
    sums = jax.ops.segment_sum(end_states, junction_ids, num_segments=NJ)
    means = sums[junction_ids] / degree[:, None, None]
    added = junction_rate * (means - end_states)
    added = jnp.transpose(added.reshape(2, pipe_count, components, columns), (0, 2, 3, 1))
    return added


def reference(directions, diag_blocks, left_blocks, right_blocks, param_blocks, obs_weight, end_junction):
    junction_ids = end_junction[:, :, 0].reshape(-1).astype(jnp.int32)
    counts = jax.ops.segment_sum(jnp.ones(junction_ids.shape, jnp.float32), junction_ids, num_segments=NJ)
    degree = counts[junction_ids]
    widths = ((0, 0), (0, 0), (0, 0))
    left_next = jnp.pad(left_blocks, widths + ((0, 1),))[..., 1:]
    right_prev = jnp.pad(right_blocks, widths + ((1, 0),))[..., :-1]

    def forward(state_in):
        padded = jnp.pad(state_in, widths + ((1, 1),))
        result = block_apply(diag_blocks, state_in, False)
        result = result + block_apply(left_blocks, padded[..., :-2], False)
        result = result + block_apply(right_blocks, padded[..., 2:], False)
        added = junction_add(state_in, junction_ids, degree)
        result = result.at[..., 0].add(added[0])
        return result.at[..., -1].add(added[1])

    def backward(state_in):
        padded = jnp.pad(state_in, widths + ((1, 1),))
        result = block_apply(diag_blocks, state_in, True)
        result = result + block_apply(left_next, padded[..., 2:], True)
        result = result + block_apply(right_prev, padded[..., :-2], True)
        added = junction_add(state_in, junction_ids, degree)
        result = result.at[..., 0].add(added[0])
        return result.at[..., -1].add(added[1])

    def solve_group(columns_in):
        source = block_apply(param_blocks, columns_in, False)
        state = source
        for step in range(STEPS - 1):
            state = forward(state) + source
        adjoint = obs_weight[:, None] * state
        hess = block_apply(param_blocks, adjoint, True)
        for step in range(STEPS - 1):
            adjoint = backward(adjoint)
            hess = hess + block_apply(param_blocks, adjoint, True)
        return hess

    npar, columns, pipe_total, length = directions.shape
    grouped = directions.reshape(npar, columns // column_group, column_group, pipe_total, length)
    grouped = jnp.transpose(grouped, (1, 0, 2, 3, 4))
    results = lax.map(solve_group, grouped)
    return jnp.transpose(results, (1, 0, 2, 3, 4)).reshape(npar, columns, pipe_total, length)
```

```python
import jax
import jax.numpy as jnp
from jax import lax
from jax.experimental import pallas as pl
from jax.experimental.pallas import tpu as pltpu
from jax.sharding import PartitionSpec as P

MESH = pl.DeviceIdType.MESH
HIGH = lax.Precision.HIGHEST
F32 = jnp.float32
X_SIZE, Z_SIZE = 4, 8
COMP, NPAR, COLS, PIPES, CELLS = 4, 2, 64, 8, 256
LANES = 128
Z_STEPS = (4, 3, 5, 2, 6, 1, 7)
PE, PN, DD, CIN, COUT, WT = 0, 8, 16, 32, 48, 64
N_COEF = 68
J_W, J_ONE, J_ID = 24, 28, 29
ROWS = 24


def iota(shape, dim):
    return lax.broadcasted_iota(jnp.int32, shape, dim)


def spread(column):
    return jnp.broadcast_to(column, (PIPES, LANES))


def kernel(
    dir_in, diag_in, left_in, right_in, par_in, wt_in, ids_in, out_ref,
    dirs, diag, left, right, par, wt, ids,
    hess, band, coef, comp, src_s, wl_s, n_send, n_recv, jbuf, mean_s, mean_a,
    in_sem, out_sem, ns_sem, nr_sem, zs_sem, zr_sem, ys_sem, yr_sem,
):
    g = lax.axis_index("region")
    s = lax.axis_index("sub")
    x, z = g // Z_SIZE, lax.rem(g, Z_SIZE)
    is_first, is_last = s == 0, s == 7
    is_end = jnp.logical_or(is_first, is_last)
    pe = s // 7

    z_peers = [(x * Z_SIZE + lax.rem(z + k, Z_SIZE), s) for k in Z_STEPS]
    xr = [lax.rem(x + k, X_SIZE) * Z_SIZE + z for k in range(X_SIZE)]
    y_peers = [(xr[2], 7 - s), (xr[1], 7 - s), (xr[3], 7 - s), (xr[2], s), (xr[1], s), (xr[3], s), (g, 7 - s)]

    def to(peer):
        return dict(device_id={"region": peer[0], "sub": peer[1]}, device_id_type=MESH)

    interior = (s > 0, s < 7)
    beside = ((g, s - 1), (g, s + 1))

    loads = [
        pltpu.make_async_copy(a, b, in_sem.at[i])
        for i, (a, b) in enumerate(
            (
                (dir_in, dirs),
                (diag_in, diag),
                (left_in, left),
                (right_in, right),
                (par_in, par),
                (wt_in, wt),
                (ids_in, ids),
            )
        )
    ]
    for load in loads:
        load.start()
    barrier = pltpu.get_barrier_semaphore()
    for side in (0, 1):

        @pl.when(interior[side])
        def _():
            pl.semaphore_signal(barrier, inc=1, **to(beside[side]))

    @pl.when(is_end)
    def _():
        for peer in z_peers + y_peers:
            pl.semaphore_signal(barrier, inc=1, **to(peer))

    for load in loads:
        load.wait()

    lane = iota((PIPES, LANES), 1)
    even = lax.rem(lane, 2) == 0
    lane2 = iota((PIPES, CELLS), 1)

    ends = jnp.logical_or(
        jnp.logical_and(lane2 == 0, is_first), jnp.logical_and(lane2 == CELLS - 1, is_last)
    )
    for c in range(COMP):
        diag[c, c] = diag[c, c] - jnp.where(ends, 0.5, 0.0)

    def gather_step(j, tiles):
        tiles = list(tiles)
        for u in range(4):
            r = j * 4 + u
            here = lane // 2 == r
            for k in range(NPAR):
                a = dirs[k, r, :, 0:LANES]
                b = dirs[k, r, :, LANES:]
                tiles[k] = jnp.where(here, pltpu.roll(a, 2 * r, 1), tiles[k])
                tiles[2 + k] = jnp.where(here, pltpu.roll(b, lax.rem(2 * r + 2, LANES), 1), tiles[2 + k])
        return tuple(tiles)

    zero = jnp.zeros((PIPES, LANES), F32)
    tiles = lax.fori_loop(0, COLS // 4, gather_step, (zero,) * 4)

    def swap(v):
        return jnp.where(even, pltpu.roll(v, LANES - 1, 1), pltpu.roll(v, 1, 1))

    def nxt(v):
        return pltpu.roll(v, LANES - 1, 1)

    def lane_pack(values):
        tile = jnp.zeros((PIPES, LANES), F32)
        for i, v in enumerate(values):
            tile = jnp.where(lane == i, v, tile)
        return tile

    for side in (0, 1):
        for k in range(NPAR):
            comp[side, k] = swap(tiles[2 + k]) if side else tiles[k]
        e, n = (CELLS - 1, CELLS - 2) if side else (0, 1)
        inner, outer = (left, right) if side else (right, left)
        for t in range(COMP):
            coef[side, WT + t] = spread(wt[t, :, e : e + 1])
            for k in range(NPAR):
                coef[side, PE + NPAR * t + k] = spread(par[t, k, :, e : e + 1])
                coef[side, PN + NPAR * t + k] = spread(par[t, k, :, n : n + 1])
            for q in range(COMP):
                coef[side, DD + COMP * t + q] = spread(diag[t, q, :, e : e + 1])
                coef[side, CIN + COMP * t + q] = spread(inner[t, q, :, e : e + 1])
                coef[side, COUT + COMP * t + q] = spread(outer[t, q, :, e : e + 1])
        source = []
        for t in range(COMP):
            total = zero
            for k in range(NPAR):
                factor = jnp.where(even, coef[side, PE + NPAR * t + k], coef[side, PN + NPAR * t + k])
                total = total + factor * comp[side, k]
            source.append(total)
        after = [nxt(v) for v in source]
        for t in range(COMP):
            total = source[t]
            for q in range(COMP):
                total = total + coef[side, DD + COMP * t + q] * source[q]
                total = total + coef[side, CIN + COMP * t + q] * after[q]
            weighted = coef[side, WT + t] * total
            src_s[side, t] = source[t]
            wl_s[side, t] = weighted
            n_send[side, t] = jnp.where(even, source[t], pltpu.roll(weighted, 1, 1))
        n_send[side, COMP] = lane_pack(
            [coef[side, COUT + i] for i in range(COMP * COMP)] + [coef[side, WT + t] for t in range(COMP)]
        )

    @pl.when(is_end)
    def _():
        row = jnp.where(is_last, ids[1], ids[0])
        row = jnp.where(g >= 16, row[:, LANES:], row[:, :LANES]).astype(F32)
        mine = lane == PIPES * lax.rem(g, 16) + iota((PIPES, LANES), 0)
        own = spread(jnp.sum(jnp.where(mine, row, 0.0), axis=1, keepdims=True))
        pack = [coef[pe, PE + i] for i in range(COMP * NPAR)]
        for near in (True, False):
            for t in range(COMP):
                for k in range(NPAR):
                    total = coef[pe, PE + NPAR * t + k] if near else zero
                    for q in range(COMP):
                        block, cell = (DD, PE) if near else (CIN, PN)
                        total = total + coef[pe, block + COMP * t + q] * coef[pe, cell + NPAR * q + k]
                    pack.append(coef[pe, WT + t] * total)
        pack += [coef[pe, WT + t] for t in range(COMP)] + [zero + 1.0, own]
        for k in range(NPAR):
            jbuf[0, 0, 8 * k : 8 * k + 8] = comp[pe, k]
        jbuf[0, 0, 16:24] = lane_pack(pack)

    expected = jnp.where(is_end, 1 + len(z_peers) + len(y_peers), 2)
    pl.semaphore_wait(barrier, expected)

    def n_copy(side):
        return pltpu.make_async_remote_copy(
            src_ref=n_send.at[side],
            dst_ref=n_recv.at[1 - side],
            send_sem=ns_sem.at[side],
            recv_sem=nr_sem.at[1 - side],
            **to(beside[side]),
        )

    def z_copy(i):
        return pltpu.make_async_remote_copy(
            src_ref=jbuf.at[0, 0], dst_ref=jbuf.at[1 + i, 0], send_sem=zs_sem, recv_sem=zr_sem.at[i], **to(z_peers[i])
        )

    def forward(i):
        for j, peer in enumerate(y_peers):
            pltpu.make_async_remote_copy(
                src_ref=jbuf.at[i, 0], dst_ref=jbuf.at[i, 1 + j], send_sem=ys_sem, recv_sem=yr_sem, **to(peer)
            ).start()

    @pl.when(is_end)
    def _():
        for i in range(len(z_peers)):
            z_copy(i).start()
        forward(0)

    for side in (0, 1):

        @pl.when(interior[side])
        def _():
            n_copy(side).start()

    def up(v):
        return jnp.where(lane2 == CELLS - 1, 0.0, pltpu.roll(v, CELLS - 1, 1))

    def down(v):
        return jnp.where(lane2 == 0, 0.0, pltpu.roll(v, 1, 1))

    p_here = [[par[t, k] for k in range(NPAR)] for t in range(COMP)]
    p_up = [[up(v) for v in vs] for vs in p_here]
    p_down = [[down(v) for v in vs] for vs in p_here]

    def product(blocks, cells, start):
        rows = []
        for t in range(COMP):
            row = []
            for k in range(NPAR):
                total = start[t][k] if start is not None else None
                for q in range(COMP):
                    term = blocks[t, q] * cells[q][k]
                    total = term if total is None else total + term
                row.append(total)
            rows.append(row)
        return rows

    b0 = product(diag, p_here, p_here)
    bm = product(left, p_down, None)
    bp = product(right, p_up, None)
    weight = [wt[t] for t in range(COMP)]
    u0 = [[weight[t] * v for v in b0[t]] for t in range(COMP)]
    um = [[weight[t] * v for v in bm[t]] for t in range(COMP)]
    upl = [[weight[t] * v for v in bp[t]] for t in range(COMP)]

    def inner_sum(a, b, k, q):
        total = a[0][k] * b[0][q]
        for t in range(1, COMP):
            total = total + a[t][k] * b[t][q]
        return total

    for k in range(NPAR):
        for q in range(NPAR):
            i = NPAR * k + q
            if k <= q:
                centre = inner_sum(b0, u0, k, q) + down(inner_sum(bp, upl, k, q)) + up(inner_sum(bm, um, k, q))
                band[8 + i] = centre
                if k != q:
                    band[8 + NPAR * q + k] = centre
            one = inner_sum(b0, upl, k, q) + up(inner_sum(bm, u0, k, q))
            two = up(inner_sum(bm, upl, k, q))
            band[12 + i] = one
            band[16 + i] = two
            band[4 + NPAR * q + k] = down(one)
            band[NPAR * q + k] = down(down(two))

    def wide_step(r, carry):
        shifted = []
        for k in range(NPAR):
            a = dirs[k, r, :, 0:LANES]
            b = dirs[k, r, :, LANES:]
            per_offset = []
            for off in (-2, -1, 0, 1, 2):
                if off == 0:
                    per_offset.append((a, b))
                    continue
                ra = pltpu.roll(a, -off % LANES, 1)
                rb = pltpu.roll(b, -off % LANES, 1)
                if off < 0:
                    per_offset.append((ra, jnp.where(lane < -off, ra, rb)))
                else:
                    per_offset.append((jnp.where(lane >= LANES - off, rb, ra), rb))
            shifted.append(per_offset)
        for half in (0, 1):
            span = slice(half * LANES, half * LANES + LANES)
            for k in range(NPAR):
                total = None
                for o in range(5):
                    for q in range(NPAR):
                        term = band[4 * o + NPAR * k + q, :, span] * shifted[q][o][half]
                        total = term if total is None else total + term
                hess[k, r, :, span] = total
        return carry

    lax.fori_loop(0, COLS, wide_step, 0)

    def finish(side):
        is_right = side == 1
        change = [coef[side, WT + t] * mean_s[side, t] for t in range(COMP)]
        at_end, at_next = [], []
        for q in range(COMP):
            total = change[q] + mean_a[side, q]
            other = zero
            for t in range(COMP):
                total = total + coef[side, DD + COMP * t + q] * change[t]
                other = other + coef[side, CIN + COMP * t + q] * change[t]
            at_end.append(total)
            at_next.append(other)
        corr = []
        for k in range(NPAR):
            c0, c1 = zero, zero
            for t in range(COMP):
                c0 = c0 + coef[side, PE + NPAR * t + k] * at_end[t]
                c1 = c1 + coef[side, PN + NPAR * t + k] * at_next[t]
            straight = jnp.where(even, c0, pltpu.roll(c1, 1, 1))
            corr.append(jnp.where(is_right, swap(straight), straight))
        edge = jnp.where(is_right, LANES - 2, 0)
        here = jnp.logical_and(lane >= edge, lane < edge + 2)
        start = side * LANES
        if not isinstance(side, int):
            start = pl.multiple_of(start, LANES)

        def add_step(j, carry):
            for u in range(4):
                r = j * 4 + u
                for k in range(NPAR):
                    moved = pltpu.roll(corr[k], lax.rem(LANES + edge - 2 * r, LANES), 1)
                    at = (k, r, slice(None), pl.ds(start, LANES))
                    hess[at] = hess[at] + jnp.where(here, moved, 0.0)
            return carry

        lax.fori_loop(0, COLS // 4, add_step, 0)
        half = (slice(None), slice(None), slice(None), pl.ds(start, LANES))
        pltpu.make_async_copy(hess.at[half], out_ref.at[half], out_sem.at[side]).start()

    @pl.when(is_end)
    def _():
        for i in reversed(range(len(z_peers))):
            z_copy(i).wait_recv()
            forward(1 + i)

    for side in (0, 1):

        @pl.when(interior[side])
        def _():
            n_copy(1 - side).wait_recv()
            theirs = n_recv[side, COMP]
            out_block = [spread(theirs[:, i : i + 1]) for i in range(COMP * COMP)]
            out_weight = [spread(theirs[:, COMP * COMP + t : COMP * COMP + t + 1]) for t in range(COMP)]
            pairs = [n_recv[side, t] for t in range(COMP)]
            adjoint = []
            for t in range(COMP):
                total, change = zero, zero
                for q in range(COMP):
                    total = total + out_block[COMP * t + q] * src_s[side, q]
                    change = change + coef[side, COUT + COMP * t + q] * pairs[q]
                adjoint.append(nxt(pairs[t]) + out_weight[t] * total)
                mean_s[side, t] = change
            for q in range(COMP):
                total = zero
                for t in range(COMP):
                    total = total + out_block[COMP * t + q] * adjoint[t]
                mean_a[side, q] = total
            finish(side)

    @pl.when(is_end)
    def _():
        tail = jbuf.at[:, pl.ds(1, 7)]
        arrived = pltpu.make_async_remote_copy(
            src_ref=tail, dst_ref=tail, send_sem=ys_sem, recv_sem=yr_sem, **to(y_peers[0])
        )
        arrived.wait_recv()
        count = 64 * PIPES
        x0 = jbuf[:, :, 0:8].reshape(count, LANES)
        x1 = jbuf[:, :, 8:16].reshape(count, LANES)
        cf = jbuf[:, :, 16:24].reshape(count, LANES)
        replicate = (iota((LANES, 2 * LANES), 0) == iota((LANES, 2 * LANES), 1) // PIPES).astype(F32)
        wide = jnp.dot(cf, replicate, precision=HIGH, preferred_element_type=F32)
        own = cf[0:8, J_ID : J_ID + 1]
        pattern = lax.rem(lane, PIPES) == iota((PIPES, LANES), 0)
        own_lane = jnp.sum(jnp.where(pattern, own, 0.0), axis=0, keepdims=True)
        same = cf[:, J_ID : J_ID + 1] == own_lane
        w0 = jnp.where(same, wide[:, :LANES], 0.0)
        w1 = jnp.where(same, wide[:, LANES:], 0.0)
        w_all = jnp.concatenate([w0, w1], axis=1)
        x_all = jnp.concatenate([x0, x1], axis=1)
        sums = jnp.dot(w_all.T, x_all, precision=HIGH, preferred_element_type=F32)
        totals = jnp.sum(w1, axis=0, keepdims=True)

        def member(i):
            at = lane == PIPES * (i - 16) + iota((PIPES, LANES), 0)
            return spread(jnp.sum(jnp.where(at, totals, 0.0), axis=1, keepdims=True))

        share = 1.0 / member(J_ONE)

        def part(c, k):
            return sums[PIPES * c : PIPES * c + PIPES, LANES * k : LANES * k + LANES]

        for t in range(COMP):
            c = NPAR * t
            mean = share * (part(c, 0) + part(c + 1, 1))
            near = part(8 + c, 0) + part(9 + c, 1)
            far = part(16 + c, 0) + part(17 + c, 1)
            mean_s[pe, t] = 0.5 * mean
            mean_a[pe, t] = 0.5 * share * (near + nxt(far) + 0.5 * member(J_W + t) * mean)
        finish(pe)
        arrived.wait_send()
        pltpu.make_async_remote_copy(
            src_ref=jbuf.at[pl.ds(0, 7), 0],
            dst_ref=jbuf.at[pl.ds(1, 7), 0],
            send_sem=zs_sem,
            recv_sem=yr_sem,
            **to(z_peers[0]),
        ).wait_send()

    for side in (0, 1):

        @pl.when(interior[side])
        def _():
            n_copy(side).wait_send()

    for side in (0, 1):
        span = pl.ds(side * LANES, LANES)
        pltpu.make_async_copy(hess.at[:, :, :, span], out_ref.at[:, :, :, span], out_sem.at[side]).wait()


def on_device(directions, diag_blocks, left_blocks, right_blocks, param_blocks, obs_weight, end_junction):
    args = (directions, diag_blocks, left_blocks, right_blocks, param_blocks, obs_weight, jnp.swapaxes(end_junction, 1, 2))
    dma = pltpu.SemaphoreType.DMA
    return pl.pallas_call(
        kernel,
        out_shape=jax.ShapeDtypeStruct(directions.shape, F32),
        in_specs=[pl.BlockSpec(memory_space=pl.ANY)] * len(args),
        out_specs=pl.BlockSpec(memory_space=pl.ANY),
        scratch_shapes=[pltpu.VMEM(a.shape, a.dtype) for a in args]
        + [
            pltpu.VMEM(directions.shape, F32),
            pltpu.VMEM((5 * NPAR * NPAR, PIPES, CELLS), F32),
            pltpu.VMEM((2, N_COEF, PIPES, LANES), F32),
            pltpu.VMEM((2, NPAR, PIPES, LANES), F32),
            pltpu.VMEM((2, COMP, PIPES, LANES), F32),
            pltpu.VMEM((2, COMP, PIPES, LANES), F32),
            pltpu.VMEM((2, COMP + 1, PIPES, LANES), F32),
            pltpu.VMEM((2, COMP + 1, PIPES, LANES), F32),
            pltpu.VMEM((8, 8, ROWS, LANES), F32),
            pltpu.VMEM((2, COMP, PIPES, LANES), F32),
            pltpu.VMEM((2, COMP, PIPES, LANES), F32),
            dma((7,)),
            dma((2,)),
            dma((2,)),
            dma((2,)),
            dma,
            dma((7,)),
            dma,
            dma,
        ],
        compiler_params=pltpu.CompilerParams(
            collective_id=3, has_side_effects=True, vmem_limit_bytes=40 * 1024 * 1024
        ),
    )(*args)


def solution(mesh):
    return jax.shard_map(
        on_device,
        mesh=mesh,
        in_specs=(
            P(None, None, "region", "sub"),
            P(None, None, "region", "sub"),
            P(None, None, "region", "sub"),
            P(None, None, "region", "sub"),
            P(None, None, "region", "sub"),
            P(None, "region", "sub"),
            P(),
        ),
        out_specs=P(None, None, "region", "sub"),
        check_vma=False,
    )
```

```python
import jax
import jax.numpy as jnp
from jax import lax
from jax.experimental import pallas as pl
from jax.experimental.pallas import tpu as pltpu
from jax.sharding import PartitionSpec as P

MESH = pl.DeviceIdType.MESH
HIGH = lax.Precision.HIGHEST
F32 = jnp.float32
X_SIZE, Z_SIZE = 4, 8
COMP, NPAR, COLS, PIPES, CELLS = 4, 2, 64, 8, 256
LANES = 128
Z_STEPS = (4, 3, 5, 2, 6, 1, 7)
PE, PN, DD, CIN, COUT, WT = 0, 8, 16, 32, 48, 64
N_COEF = 68
J_W, J_ONE, J_ID = 24, 28, 29
ROWS = 24


def iota(shape, dim):
    return lax.broadcasted_iota(jnp.int32, shape, dim)


def spread(column):
    return jnp.broadcast_to(column, (PIPES, LANES))


def kernel(
    dir_in, diag_in, left_in, right_in, par_in, wt_in, ids_in, hess,
    dirs, diag, left, right, par, wt, ids,
    band, coef, comp, src_s, n_send, n_recv, jbuf, mean_s, mean_a,
    dir_sem, in_sem, ns_sem, nr_sem, zs_sem, zr_sem, ys_sem, yr_sem,
):
    g = lax.axis_index("region")
    s = lax.axis_index("sub")
    x, z = g // Z_SIZE, lax.rem(g, Z_SIZE)
    is_first, is_last = s == 0, s == 7
    is_end = jnp.logical_or(is_first, is_last)
    pe = s // 7

    z_peers = [(x * Z_SIZE + lax.rem(z + k, Z_SIZE), s) for k in Z_STEPS]
    xr = [lax.rem(x + k, X_SIZE) * Z_SIZE + z for k in range(X_SIZE)]
    y_peers = [(xr[2], 7 - s), (xr[1], 7 - s), (xr[3], 7 - s), (xr[2], s), (xr[1], s), (xr[3], s), (g, 7 - s)]

    def to(peer):
        return dict(device_id={"region": peer[0], "sub": peer[1]}, device_id_type=MESH)

    interior = (s > 0, s < 7)
    beside = ((g, s - 1), (g, s + 1))

    def half_load(half):
        start = pl.multiple_of(half * LANES, LANES)
        return pltpu.make_async_copy(dir_in.at[:, :, :, pl.ds(start, LANES)], dirs.at[half], dir_sem.at[half])

    loads = [
        pltpu.make_async_copy(a, b, in_sem.at[i])
        for i, (a, b) in enumerate(
            ((par_in, par), (diag_in, diag), (wt_in, wt), (left_in, left), (right_in, right), (ids_in, ids))
        )
    ]
    half_load(pe).start()
    for load in loads:
        load.start()
    barrier = pltpu.get_barrier_semaphore()

    @pl.when(is_end)
    def _():
        for peer in z_peers + y_peers:
            pl.semaphore_signal(barrier, inc=1, **to(peer))

    for side in (0, 1):

        @pl.when(interior[side])
        def _():
            pl.semaphore_signal(barrier, inc=1, **to(beside[side]))

    half_load(1 - pe).start()
    for load in loads:
        load.wait()

    lane = iota((PIPES, LANES), 1)
    even = lax.rem(lane, 2) == 0
    lane2 = iota((PIPES, CELLS), 1)
    zero = jnp.zeros((PIPES, LANES), F32)

    ends = jnp.logical_or(
        jnp.logical_and(lane2 == 0, is_first), jnp.logical_and(lane2 == CELLS - 1, is_last)
    )
    for c in range(COMP):
        diag[c, c] = diag[c, c] - jnp.where(ends, 0.5, 0.0)

    def swap(v):
        return jnp.where(even, pltpu.roll(v, LANES - 1, 1), pltpu.roll(v, 1, 1))

    def nxt(v):
        return pltpu.roll(v, LANES - 1, 1)

    def lane_pack(values):
        tile = zero
        for i, v in enumerate(values):
            tile = jnp.where(lane == i, v, tile)
        return tile

    def end_cells(side):
        def step(j, tiles):
            tiles = list(tiles)
            for u in range(4):
                r = j * 4 + u
                shift = lax.rem(2 * r + 2 * side, LANES)
                for k in range(NPAR):
                    tiles[k] = jnp.where(lane // 2 == r, pltpu.roll(dirs[side, k, r], shift, 1), tiles[k])
            return tuple(tiles)

        tiles = lax.fori_loop(0, COLS // 4, step, (zero,) * NPAR, unroll=4)
        for k in range(NPAR):
            comp[side, k] = swap(tiles[k]) if side else tiles[k]
        e, n = (CELLS - 1, CELLS - 2) if side else (0, 1)
        inner, outer = (left, right) if side else (right, left)
        for t in range(COMP):
            coef[side, WT + t] = spread(wt[t, :, e : e + 1])
            for k in range(NPAR):
                coef[side, PE + NPAR * t + k] = spread(par[t, k, :, e : e + 1])
                coef[side, PN + NPAR * t + k] = spread(par[t, k, :, n : n + 1])
            for q in range(COMP):
                coef[side, DD + COMP * t + q] = spread(diag[t, q, :, e : e + 1])
                coef[side, CIN + COMP * t + q] = spread(inner[t, q, :, e : e + 1])
                coef[side, COUT + COMP * t + q] = spread(outer[t, q, :, e : e + 1])

    @pl.when(is_end)
    def _():
        half_load(pe).wait()

    for side, chosen in ((0, is_first), (1, is_last)):

        @pl.when(chosen)
        def _():
            end_cells(side)
            row = jnp.where(g >= 16, ids[side, :, LANES:], ids[side, :, :LANES]).astype(F32)
            mine = lane == PIPES * lax.rem(g, 16) + iota((PIPES, LANES), 0)
            own = spread(jnp.sum(jnp.where(mine, row, 0.0), axis=1, keepdims=True))
            pack = [coef[side, PE + i] for i in range(COMP * NPAR)]
            for near in (True, False):
                for t in range(COMP):
                    for k in range(NPAR):
                        total = coef[side, PE + NPAR * t + k] if near else zero
                        for q in range(COMP):
                            block, cell = (DD, PE) if near else (CIN, PN)
                            total = total + coef[side, block + COMP * t + q] * coef[side, cell + NPAR * q + k]
                        pack.append(coef[side, WT + t] * total)
            pack += [coef[side, WT + t] for t in range(COMP)] + [zero + 1.0, own]
            for k in range(NPAR):
                jbuf[0, 0, 8 * k : 8 * k + 8] = comp[side, k]
            jbuf[0, 0, 16:24] = lane_pack(pack)

    expected = jnp.where(is_end, 1 + len(z_peers) + len(y_peers), 2)
    pl.semaphore_wait(barrier, expected)

    def n_copy(side):
        return pltpu.make_async_remote_copy(
            src_ref=n_send.at[side],
            dst_ref=n_recv.at[1 - side],
            send_sem=ns_sem.at[side],
            recv_sem=nr_sem.at[1 - side],
            **to(beside[side]),
        )

    def z_copy(i):
        return pltpu.make_async_remote_copy(
            src_ref=jbuf.at[0, 0], dst_ref=jbuf.at[1 + i, 0], send_sem=zs_sem, recv_sem=zr_sem.at[i], **to(z_peers[i])
        )

    def forward(i):
        for j, peer in enumerate(y_peers):
            pltpu.make_async_remote_copy(
                src_ref=jbuf.at[i, 0], dst_ref=jbuf.at[i, 1 + j], send_sem=ys_sem, recv_sem=yr_sem, **to(peer)
            ).start()

    @pl.when(is_end)
    def _():
        for i in range(len(z_peers)):
            z_copy(i).start()
        forward(0)

    half_load(1 - pe).wait()

    @pl.when(jnp.logical_not(is_end))
    def _():
        half_load(pe).wait()

    for side in (0, 1):

        @pl.when(interior[side])
        def _():
            end_cells(side)
            source = []
            for t in range(COMP):
                total = zero
                for k in range(NPAR):
                    factor = jnp.where(even, coef[side, PE + NPAR * t + k], coef[side, PN + NPAR * t + k])
                    total = total + factor * comp[side, k]
                source.append(total)
            after = [nxt(v) for v in source]
            for t in range(COMP):
                total = source[t]
                for q in range(COMP):
                    total = total + coef[side, DD + COMP * t + q] * source[q]
                    total = total + coef[side, CIN + COMP * t + q] * after[q]
                src_s[side, t] = source[t]
                n_send[side, t] = jnp.where(even, source[t], pltpu.roll(coef[side, WT + t] * total, 1, 1))
            n_send[side, COMP] = lane_pack(
                [coef[side, COUT + i] for i in range(COMP * COMP)] + [coef[side, WT + t] for t in range(COMP)]
            )
            n_copy(side).start()

    def up(v):
        return jnp.where(lane2 == CELLS - 1, 0.0, pltpu.roll(v, CELLS - 1, 1))

    def down(v):
        return jnp.where(lane2 == 0, 0.0, pltpu.roll(v, 1, 1))

    p_here = [[par[t, k] for k in range(NPAR)] for t in range(COMP)]
    p_up = [[up(v) for v in vs] for vs in p_here]
    p_down = [[down(v) for v in vs] for vs in p_here]

    def product(blocks, cells, start):
        rows = []
        for t in range(COMP):
            row = []
            for k in range(NPAR):
                total = start[t][k] if start is not None else None
                for q in range(COMP):
                    term = blocks[t, q] * cells[q][k]
                    total = term if total is None else total + term
                row.append(total)
            rows.append(row)
        return rows

    b0 = product(diag, p_here, p_here)
    bm = product(left, p_down, None)
    bp = product(right, p_up, None)
    weight = [wt[t] for t in range(COMP)]
    u0 = [[weight[t] * v for v in b0[t]] for t in range(COMP)]
    um = [[weight[t] * v for v in bm[t]] for t in range(COMP)]
    upl = [[weight[t] * v for v in bp[t]] for t in range(COMP)]

    def inner_sum(a, b, k, q):
        total = a[0][k] * b[0][q]
        for t in range(1, COMP):
            total = total + a[t][k] * b[t][q]
        return total

    for k in range(NPAR):
        for q in range(NPAR):
            i = NPAR * k + q
            if k <= q:
                centre = inner_sum(b0, u0, k, q) + down(inner_sum(bp, upl, k, q)) + up(inner_sum(bm, um, k, q))
                band[8 + i] = centre
                if k != q:
                    band[8 + NPAR * q + k] = centre
            one = inner_sum(b0, upl, k, q) + up(inner_sum(bm, u0, k, q))
            two = up(inner_sum(bm, upl, k, q))
            band[12 + i] = one
            band[16 + i] = two
            band[4 + NPAR * q + k] = down(one)
            band[NPAR * q + k] = down(down(two))

    def wide_step(r, carry):
        shifted = []
        for k in range(NPAR):
            a = dirs[0, k, r]
            b = dirs[1, k, r]
            per_offset = []
            for off in (-2, -1, 0, 1, 2):
                if off == 0:
                    per_offset.append((a, b))
                    continue
                ra = pltpu.roll(a, -off % LANES, 1)
                rb = pltpu.roll(b, -off % LANES, 1)
                if off < 0:
                    per_offset.append((ra, jnp.where(lane < -off, ra, rb)))
                else:
                    per_offset.append((jnp.where(lane >= LANES - off, rb, ra), rb))
            shifted.append(per_offset)
        for half in (0, 1):
            span = slice(half * LANES, half * LANES + LANES)
            for k in range(NPAR):
                total = None
                for o in range(5):
                    for q in range(NPAR):
                        term = band[4 * o + NPAR * k + q, :, span] * shifted[q][o][half]
                        total = term if total is None else total + term
                hess[k, r, :, span] = total
        return carry

    lax.fori_loop(0, COLS, wide_step, 0, unroll=4)

    def finish(side):
        is_right = side == 1
        change = [coef[side, WT + t] * mean_s[side, t] for t in range(COMP)]
        at_end, at_next = [], []
        for q in range(COMP):
            total = change[q] + mean_a[side, q]
            other = zero
            for t in range(COMP):
                total = total + coef[side, DD + COMP * t + q] * change[t]
                other = other + coef[side, CIN + COMP * t + q] * change[t]
            at_end.append(total)
            at_next.append(other)
        corr = []
        for k in range(NPAR):
            c0, c1 = zero, zero
            for t in range(COMP):
                c0 = c0 + coef[side, PE + NPAR * t + k] * at_end[t]
                c1 = c1 + coef[side, PN + NPAR * t + k] * at_next[t]
            straight = jnp.where(even, c0, pltpu.roll(c1, 1, 1))
            corr.append(jnp.where(is_right, swap(straight), straight))
        edge = jnp.where(is_right, LANES - 2, 0)
        here = jnp.logical_and(lane >= edge, lane < edge + 2)
        start = side * LANES
        if not isinstance(side, int):
            start = pl.multiple_of(start, LANES)

        def add_step(j, carry):
            for u in range(4):
                r = j * 4 + u
                for k in range(NPAR):
                    moved = pltpu.roll(corr[k], lax.rem(LANES + edge - 2 * r, LANES), 1)
                    at = (k, r, slice(None), pl.ds(start, LANES))
                    hess[at] = hess[at] + jnp.where(here, moved, 0.0)
            return carry

        lax.fori_loop(0, COLS // 4, add_step, 0, unroll=4)

    @pl.when(is_end)
    def _():
        for i in reversed(range(len(z_peers))):
            z_copy(i).wait_recv()
            forward(1 + i)

    for side in (0, 1):

        @pl.when(interior[side])
        def _():
            n_copy(1 - side).wait_recv()
            theirs = n_recv[side, COMP]
            out_block = [spread(theirs[:, i : i + 1]) for i in range(COMP * COMP)]
            out_weight = [spread(theirs[:, COMP * COMP + t : COMP * COMP + t + 1]) for t in range(COMP)]
            pairs = [n_recv[side, t] for t in range(COMP)]
            adjoint = []
            for t in range(COMP):
                total, change = zero, zero
                for q in range(COMP):
                    total = total + out_block[COMP * t + q] * src_s[side, q]
                    change = change + coef[side, COUT + COMP * t + q] * pairs[q]
                adjoint.append(nxt(pairs[t]) + out_weight[t] * total)
                mean_s[side, t] = change
            for q in range(COMP):
                total = zero
                for t in range(COMP):
                    total = total + out_block[COMP * t + q] * adjoint[t]
                mean_a[side, q] = total
            finish(side)

    @pl.when(is_end)
    def _():
        tail = jbuf.at[:, pl.ds(1, 7)]
        arrived = pltpu.make_async_remote_copy(
            src_ref=tail, dst_ref=tail, send_sem=ys_sem, recv_sem=yr_sem, **to(y_peers[0])
        )
        arrived.wait_recv()
        count = 64 * PIPES
        x_all = jnp.concatenate([jbuf[:, :, 0:8].reshape(count, LANES), jbuf[:, :, 8:16].reshape(count, LANES)], axis=1)
        coefs = jbuf[:, :, 16:24].reshape(count, LANES).T
        own = spread(jbuf[0, 0, 16:24, J_ID : J_ID + 1])[:, 0:1]
        same = coefs[J_ID : J_ID + 1] == own
        rows = [jnp.where(same, coefs[i : i + 1], 0.0) for i in range(J_ONE + 1)]
        sums = jnp.dot(jnp.concatenate(rows[:J_W]), x_all, precision=HIGH, preferred_element_type=F32)

        def member(i):
            return spread(jnp.sum(rows[i], axis=1, keepdims=True))

        share = 1.0 / member(J_ONE)

        def part(c, k):
            return sums[PIPES * c : PIPES * c + PIPES, LANES * k : LANES * k + LANES]

        for t in range(COMP):
            c = NPAR * t
            mean = share * (part(c, 0) + part(c + 1, 1))
            near = part(8 + c, 0) + part(9 + c, 1)
            far = part(16 + c, 0) + part(17 + c, 1)
            mean_s[pe, t] = 0.5 * mean
            mean_a[pe, t] = 0.5 * share * (near + nxt(far) + 0.5 * member(J_W + t) * mean)
        finish(pe)
        arrived.wait_send()
        pltpu.make_async_remote_copy(
            src_ref=jbuf.at[pl.ds(0, 7), 0],
            dst_ref=jbuf.at[pl.ds(1, 7), 0],
            send_sem=zs_sem,
            recv_sem=yr_sem,
            **to(z_peers[0]),
        ).wait_send()

    for side in (0, 1):

        @pl.when(interior[side])
        def _():
            n_copy(side).wait_send()


def on_device(directions, diag_blocks, left_blocks, right_blocks, param_blocks, obs_weight, end_junction):
    args = (directions, diag_blocks, left_blocks, right_blocks, param_blocks, obs_weight, jnp.swapaxes(end_junction, 1, 2))
    args = tuple(pltpu.with_memory_space_constraint(a, pltpu.HBM) for a in args)
    dma = pltpu.SemaphoreType.DMA

    def tiles(*counts):
        return pltpu.VMEM(counts + (PIPES, LANES), F32)

    return pl.pallas_call(
        kernel,
        out_shape=pltpu.VMEM(directions.shape, F32),
        in_specs=[pl.BlockSpec(memory_space=pl.ANY)] * len(args),
        out_specs=pl.BlockSpec(memory_space=pltpu.VMEM),
        scratch_shapes=[tiles(2, NPAR, COLS)]
        + [pltpu.VMEM(a.shape, a.dtype) for a in args[1:]]
        + [
            pltpu.VMEM((5 * NPAR * NPAR, PIPES, CELLS), F32),
            tiles(2, N_COEF),
            tiles(2, NPAR),
            tiles(2, COMP),
            tiles(2, COMP + 1),
            tiles(2, COMP + 1),
            pltpu.VMEM((8, 8, ROWS, LANES), F32),
            tiles(2, COMP),
            tiles(2, COMP),
            dma((2,)),
            dma((6,)),
            dma((2,)),
            dma((2,)),
            dma,
            dma((7,)),
            dma,
            dma,
        ],
        compiler_params=pltpu.CompilerParams(
            collective_id=3, has_side_effects=True, vmem_limit_bytes=56 * 1024 * 1024
        ),
    )(*args)


def solution(mesh):
    return jax.shard_map(
        on_device,
        mesh=mesh,
        in_specs=(
            P(None, None, "region", "sub"),
            P(None, None, "region", "sub"),
            P(None, None, "region", "sub"),
            P(None, None, "region", "sub"),
            P(None, None, "region", "sub"),
            P(None, "region", "sub"),
            P(),
        ),
        out_specs=P(None, None, "region", "sub"),
        check_vma=False,
    )
```

```python
import jax
import jax.numpy as jnp
from jax import lax
from jax.experimental import pallas as pl
from jax.experimental.pallas import tpu as pltpu
from jax.sharding import PartitionSpec as P

MESH = pl.DeviceIdType.MESH
F32 = jnp.float32
BF16 = jnp.bfloat16
X_SIZE, Z_SIZE = 4, 8
COMP, NPAR, COLS, PIPES, CELLS = 4, 2, 64, 8, 256
LANES = 128
Z_STEPS = (4, 3, 5, 2, 6, 1, 7)
PE, PN, DD, CIN, COUT, WT = 0, 8, 16, 32, 48, 64
N_COEF = 68
J_W, J_ID, J_SPAN = 24, 28, 32
ROWS = 18


def iota(shape, dim):
    return lax.broadcasted_iota(jnp.int32, shape, dim)


def split(v, kind=BF16):
    parts = []
    for _ in range(3):
        part = v.astype(BF16)
        v = v - part.astype(F32)
        parts.append(part.astype(kind))
    return parts


def spread(column):
    return jnp.broadcast_to(column, (PIPES, LANES))


def kernel(
    dir_in, diag_in, left_in, right_in, par_in, wt_in, ids_in, hess,
    dirs, diag, left, right, par, wt, ids,
    band, coef, comp, src_s, n_send, n_recv, jbuf, j_sum, j_weight, j_own, mean_s, mean_a,
    dir_sem, in_sem, ns_sem, nr_sem, zs_sem, zr_sem, ys_sem, yr_sem,
):
    g = lax.axis_index("region")
    s = lax.axis_index("sub")
    x, z = g // Z_SIZE, lax.rem(g, Z_SIZE)
    me = 2 * x + s // 7
    is_first, is_last = s == 0, s == 7
    is_end = jnp.logical_or(is_first, is_last)
    early = jnp.logical_and(is_end, z < Z_SIZE // 2)
    pe = s // 7

    z_peers = [(x * Z_SIZE + lax.rem(z + k, Z_SIZE), s) for k in Z_STEPS]
    xr = [lax.rem(x + k, X_SIZE) * Z_SIZE + z for k in range(X_SIZE)]
    y_peers = [(xr[2], 7 - s), (xr[1], 7 - s), (xr[3], 7 - s), (xr[2], s), (xr[1], s), (xr[3], s), (g, 7 - s)]

    def to(peer):
        return dict(device_id={"region": peer[0], "sub": peer[1]}, device_id_type=MESH)

    interior = (s > 0, s < 7)
    beside = ((g, s - 1), (g, s + 1))

    def half_load(half):
        start = pl.multiple_of(half * LANES, LANES)
        return pltpu.make_async_copy(dir_in.at[:, :, :, pl.ds(start, LANES)], dirs.at[half], dir_sem.at[half])

    loads = [
        pltpu.make_async_copy(a, b, in_sem.at[i])
        for i, (a, b) in enumerate(
            ((par_in, par), (diag_in, diag), (wt_in, wt), (left_in, left), (right_in, right), (ids_in, ids))
        )
    ]
    barrier = pltpu.get_barrier_semaphore()

    @pl.when(is_end)
    def _():
        for peer in z_peers + y_peers:
            pl.semaphore_signal(barrier, inc=1, **to(peer))

    for side in (0, 1):

        @pl.when(interior[side])
        def _():
            pl.semaphore_signal(barrier, inc=1, **to(beside[side]))

    half_load(pe).start()
    for load in loads:
        load.start()
    half_load(1 - pe).start()
    for load in loads:
        load.wait()

    lane = iota((PIPES, LANES), 1)
    even = lax.rem(lane, 2) == 0
    lane2 = iota((PIPES, CELLS), 1)
    quarter = lax.rem(iota((PIPES, LANES), 0), 4)
    zero = jnp.zeros((PIPES, LANES), F32)

    ends = jnp.logical_or(
        jnp.logical_and(lane2 == 0, is_first), jnp.logical_and(lane2 == CELLS - 1, is_last)
    )
    for c in range(COMP):
        diag[c, c] = diag[c, c] - jnp.where(ends, 0.5, 0.0)

    def swap(v):
        return jnp.where(even, pltpu.roll(v, LANES - 1, 1), pltpu.roll(v, 1, 1))

    def nxt(v):
        return pltpu.roll(v, LANES - 1, 1)

    def lane_pack(values):
        tile = zero
        for i, v in enumerate(values):
            tile = jnp.where(lane == i, v, tile)
        return tile

    def end_cells(side):
        def step(j, tiles):
            tiles = list(tiles)
            for u in range(4):
                r = j * 4 + u
                shift = lax.rem(2 * r + 2 * side, LANES)
                for k in range(NPAR):
                    tiles[k] = jnp.where(lane // 2 == r, pltpu.roll(dirs[side, k, r], shift, 1), tiles[k])
            return tuple(tiles)

        tiles = lax.fori_loop(0, COLS // 4, step, (zero,) * NPAR, unroll=4)
        for k in range(NPAR):
            comp[side, k] = swap(tiles[k]) if side else tiles[k]
        e, n = (CELLS - 1, CELLS - 2) if side else (0, 1)
        inner, outer = (left, right) if side else (right, left)
        for t in range(COMP):
            coef[side, WT + t] = spread(wt[t, :, e : e + 1])
            for k in range(NPAR):
                coef[side, PE + NPAR * t + k] = spread(par[t, k, :, e : e + 1])
                coef[side, PN + NPAR * t + k] = spread(par[t, k, :, n : n + 1])
            for q in range(COMP):
                coef[side, DD + COMP * t + q] = spread(diag[t, q, :, e : e + 1])
                coef[side, CIN + COMP * t + q] = spread(inner[t, q, :, e : e + 1])
                coef[side, COUT + COMP * t + q] = spread(outer[t, q, :, e : e + 1])

    @pl.when(is_end)
    def _():
        half_load(pe).wait()

    for side, chosen in ((0, is_first), (1, is_last)):

        @pl.when(chosen)
        def _():
            end_cells(side)
            row = jnp.where(g >= 16, ids[side, :, LANES:], ids[side, :, :LANES]).astype(F32)
            mine = lane == PIPES * lax.rem(g, 16) + iota((PIPES, LANES), 0)
            own = spread(jnp.sum(jnp.where(mine, row, 0.0), axis=1, keepdims=True))
            pack = [coef[side, PE + i] for i in range(COMP * NPAR)]
            for near in (True, False):
                for t in range(COMP):
                    for k in range(NPAR):
                        total = coef[side, PE + NPAR * t + k] if near else zero
                        for q in range(COMP):
                            block, cell = (DD, PE) if near else (CIN, PN)
                            total = total + coef[side, block + COMP * t + q] * coef[side, cell + NPAR * q + k]
                        pack.append(coef[side, WT + t] * total)
            pack += [coef[side, WT + t] for t in range(COMP)] + [own]
            for k in range(NPAR):
                jbuf[z, me, 8 * k : 8 * k + 8] = comp[side, k]
            tile = lane_pack(pack)
            for m in range(1, 4):
                tile = jnp.where(quarter == m, pltpu.roll(tile, J_SPAN * m, 1), tile)
            for m in range(2):
                jbuf[z, me, 16 + m : 17 + m] = jnp.sum(tile[4 * m : 4 * m + 4], axis=0, keepdims=True)
            j_own[...] = own

    def n_copy(side):
        return pltpu.make_async_remote_copy(
            src_ref=n_send.at[side],
            dst_ref=n_recv.at[1 - side],
            send_sem=ns_sem.at[side],
            recv_sem=nr_sem.at[1 - side],
            **to(beside[side]),
        )

    def slot(plane):
        return jbuf.at[plane, me, pl.ds(0, ROWS)]

    def z_copy(plane, peer):
        return pltpu.make_async_remote_copy(
            src_ref=slot(plane), dst_ref=slot(plane), send_sem=zs_sem, recv_sem=zr_sem.at[plane], **to(peer)
        )

    def forward(plane):
        for peer in y_peers:
            pltpu.make_async_remote_copy(
                src_ref=slot(plane), dst_ref=slot(plane), send_sem=ys_sem, recv_sem=yr_sem.at[plane], **to(peer)
            ).start()

    def prepare():
        half_load(1 - pe).wait()

        @pl.when(jnp.logical_not(is_end))
        def _():
            half_load(pe).wait()

        for side in (0, 1):

            @pl.when(interior[side])
            def _():
                end_cells(side)
                source = []
                for t in range(COMP):
                    total = zero
                    for k in range(NPAR):
                        factor = jnp.where(even, coef[side, PE + NPAR * t + k], coef[side, PN + NPAR * t + k])
                        total = total + factor * comp[side, k]
                    source.append(total)
                after = [nxt(v) for v in source]
                for t in range(COMP):
                    total = source[t]
                    for q in range(COMP):
                        total = total + coef[side, DD + COMP * t + q] * source[q]
                        total = total + coef[side, CIN + COMP * t + q] * after[q]
                    src_s[side, t] = source[t]
                    n_send[side, t] = jnp.where(even, source[t], pltpu.roll(coef[side, WT + t] * total, 1, 1))
                n_send[side, COMP] = lane_pack(
                    [coef[side, COUT + i] for i in range(COMP * COMP)] + [coef[side, WT + t] for t in range(COMP)]
                )

    def piece():
        def up(v):
            return jnp.where(lane2 == CELLS - 1, 0.0, pltpu.roll(v, CELLS - 1, 1))

        def down(v):
            return jnp.where(lane2 == 0, 0.0, pltpu.roll(v, 1, 1))

        p_here = [[par[t, k] for k in range(NPAR)] for t in range(COMP)]
        p_up = [[up(v) for v in vs] for vs in p_here]
        p_down = [[down(v) for v in vs] for vs in p_here]

        def product(blocks, cells, start):
            rows = []
            for t in range(COMP):
                row = []
                for k in range(NPAR):
                    total = start[t][k] if start is not None else None
                    for q in range(COMP):
                        term = blocks[t, q] * cells[q][k]
                        total = term if total is None else total + term
                    row.append(total)
                rows.append(row)
            return rows

        b0 = product(diag, p_here, p_here)
        bm = product(left, p_down, None)
        bp = product(right, p_up, None)
        weight = [wt[t] for t in range(COMP)]
        u0 = [[weight[t] * v for v in b0[t]] for t in range(COMP)]
        um = [[weight[t] * v for v in bm[t]] for t in range(COMP)]
        upl = [[weight[t] * v for v in bp[t]] for t in range(COMP)]

        def inner_sum(a, b, k, q):
            total = a[0][k] * b[0][q]
            for t in range(1, COMP):
                total = total + a[t][k] * b[t][q]
            return total

        for k in range(NPAR):
            for q in range(NPAR):
                i = NPAR * k + q
                if k <= q:
                    centre = inner_sum(b0, u0, k, q) + down(inner_sum(bp, upl, k, q)) + up(inner_sum(bm, um, k, q))
                    band[8 + i] = centre
                    if k != q:
                        band[8 + NPAR * q + k] = centre
                one = inner_sum(b0, upl, k, q) + up(inner_sum(bm, u0, k, q))
                two = up(inner_sum(bm, upl, k, q))
                band[12 + i] = one
                band[16 + i] = two
                band[4 + NPAR * q + k] = down(one)
                band[NPAR * q + k] = down(down(two))

        def wide_step(r, carry):
            shifted = []
            for k in range(NPAR):
                a = dirs[0, k, r]
                b = dirs[1, k, r]
                per_offset = []
                for off in (-2, -1, 0, 1, 2):
                    if off == 0:
                        per_offset.append((a, b))
                        continue
                    ra = pltpu.roll(a, -off % LANES, 1)
                    rb = pltpu.roll(b, -off % LANES, 1)
                    if off < 0:
                        per_offset.append((ra, jnp.where(lane < -off, ra, rb)))
                    else:
                        per_offset.append((jnp.where(lane >= LANES - off, rb, ra), rb))
                shifted.append(per_offset)
            for half in (0, 1):
                span = slice(half * LANES, half * LANES + LANES)
                for k in range(NPAR):
                    total = None
                    for o in range(5):
                        for q in range(NPAR):
                            term = band[4 * o + NPAR * k + q, :, span] * shifted[q][o][half]
                            total = term if total is None else total + term
                    hess[k, r, :, span] = total
            return carry

        lax.fori_loop(0, COLS, wide_step, 0, unroll=4)

    @pl.when(early)
    def _():
        prepare()
        piece()

    expected = jnp.where(is_end, 1 + len(z_peers) + len(y_peers), 2)
    pl.semaphore_wait(barrier, expected)

    @pl.when(is_end)
    def _():
        for peer in z_peers:
            z_copy(z, peer).start()
        forward(z)

    @pl.when(jnp.logical_not(early))
    def _():
        prepare()

    for side in (0, 1):

        @pl.when(interior[side])
        def _():
            n_copy(side).start()

    @pl.when(jnp.logical_not(early))
    def _():
        piece()

    def finish(side):
        change = [coef[side, WT + t] * mean_s[side, t] for t in range(COMP)]
        at_end, at_next = [], []
        for q in range(COMP):
            total = change[q] + mean_a[side, q]
            other = zero
            for t in range(COMP):
                total = total + coef[side, DD + COMP * t + q] * change[t]
                other = other + coef[side, CIN + COMP * t + q] * change[t]
            at_end.append(total)
            at_next.append(other)
        corr = []
        for k in range(NPAR):
            c0, c1 = zero, zero
            for t in range(COMP):
                c0 = c0 + coef[side, PE + NPAR * t + k] * at_end[t]
                c1 = c1 + coef[side, PN + NPAR * t + k] * at_next[t]
            straight = jnp.where(even, c0, pltpu.roll(c1, 1, 1))
            corr.append(swap(straight) if side else straight)
        edge = LANES - 2 if side else 0
        here = jnp.logical_and(lane >= edge, lane < edge + 2)
        span = slice(side * LANES, side * LANES + LANES)
        for r in range(COLS):
            for k in range(NPAR):
                moved = pltpu.roll(corr[k], (LANES + edge - 2 * r) % LANES, 1)
                hess[k, r, :, span] = hess[k, r, :, span] + jnp.where(here, moved, 0.0)

    @pl.when(is_end)
    def _():
        for k in reversed(Z_STEPS):
            plane = lax.rem(z + Z_SIZE - k, Z_SIZE)
            z_copy(plane, z_peers[0]).wait_recv()
            forward(plane)

    for side in (0, 1):

        @pl.when(interior[side])
        def _():
            n_copy(1 - side).wait_recv()
            theirs = n_recv[side, COMP]
            out_block = [spread(theirs[:, i : i + 1]) for i in range(COMP * COMP)]
            out_weight = [spread(theirs[:, COMP * COMP + t : COMP * COMP + t + 1]) for t in range(COMP)]
            pairs = [n_recv[side, t] for t in range(COMP)]
            adjoint = []
            for t in range(COMP):
                total, change = zero, zero
                for q in range(COMP):
                    total = total + out_block[COMP * t + q] * src_s[side, q]
                    change = change + coef[side, COUT + COMP * t + q] * pairs[q]
                adjoint.append(nxt(pairs[t]) + out_weight[t] * total)
                mean_s[side, t] = change
            for q in range(COMP):
                total = zero
                for t in range(COMP):
                    total = total + out_block[COMP * t + q] * adjoint[t]
                mean_a[side, q] = total
            finish(side)

    @pl.when(is_end)
    def _():
        own = j_own[...]
        rows = 8 * PIPES

        def arrivals(planes, sem):
            span = jbuf.at[planes, pl.ds(0, 7), pl.ds(0, ROWS)]
            return pltpu.make_async_remote_copy(
                src_ref=span, dst_ref=span, send_sem=ys_sem, recv_sem=yr_sem.at[sem], **to(y_peers[0])
            )

        j_sum[...] = jnp.zeros_like(j_sum)
        j_weight[...] = jnp.zeros_like(j_weight)
        degree = zero
        for end in (0, 1):
            for half in (0, 1):
                row = ids[end, :, half * LANES : half * LANES + LANES].astype(F32)
                degree = degree + jnp.where(row == own, 1.0, 0.0)
        share = 1.0 / spread(jnp.sum(degree, axis=1, keepdims=True))

        def add_planes(j, carry):
            pair = [lax.rem(z + Z_SIZE - j, Z_SIZE), lax.rem(z + 1 + j, Z_SIZE)]
            columns, tiles = [], []
            for plane in pair:
                arrivals(plane, plane).wait_recv()
                columns.append([jbuf[plane, :, 8 * k : 8 * k + 8].reshape(rows, LANES) for k in range(NPAR)])
                for q in range(8):
                    packed = jnp.where(
                        iota((PIPES, LANES), 0) < 4, jbuf[plane, q, 16:17], jbuf[plane, q, 17:18]
                    )
                    tile = packed
                    for m in range(1, 4):
                        tile = jnp.where(quarter == m, pltpu.roll(packed, LANES - J_SPAN * m, 1), tile)
                    tiles.append(tile)
            x_parts = split(jnp.concatenate([jnp.concatenate(c, axis=1) for c in columns]))
            coefs = jnp.concatenate(tiles).T
            same = coefs[J_ID : J_ID + 1] == own[:, 0:1]
            w_parts = [
                jnp.concatenate([jnp.where(same, v[i : i + 1], 0.0) for i in range(J_W)]).astype(BF16)
                for v in split(coefs[:J_SPAN], F32)
            ]
            order = ((0, 0), (0, 1), (1, 0), (0, 2), (2, 0), (1, 1))
            j_sum[...] += jnp.dot(
                jnp.concatenate([w_parts[i] for i, _ in order], axis=1),
                jnp.concatenate([x_parts[i] for _, i in order]),
                preferred_element_type=F32,
            )
            for t in range(COMP):
                j_weight[t] += jnp.where(same, coefs[J_W + t : J_W + t + 1], 0.0)
            return carry

        lax.fori_loop(0, Z_SIZE // 2, add_planes, 0)

        def part(c, k):
            return j_sum[PIPES * c : PIPES * c + PIPES, LANES * k : LANES * k + LANES]

        for t in range(COMP):
            c = NPAR * t
            mean = share * (part(c, 0) + part(c + 1, 1))
            near = part(8 + c, 0) + part(9 + c, 1)
            far = part(16 + c, 0) + part(17 + c, 1)
            weights = spread(jnp.sum(j_weight[t], axis=1, keepdims=True))
            mean_s[pe, t] = 0.5 * mean
            mean_a[pe, t] = 0.5 * share * (near + nxt(far) + 0.5 * weights * mean)
        for side, chosen in ((0, is_first), (1, is_last)):

            @pl.when(chosen)
            def _():
                finish(side)

        arrivals(slice(None), 0).wait_send()
        span = jbuf.at[0, pl.ds(0, 7), pl.ds(0, ROWS)]
        pltpu.make_async_remote_copy(
            src_ref=span, dst_ref=span, send_sem=zs_sem, recv_sem=yr_sem.at[0], **to(z_peers[0])
        ).wait_send()

    for side in (0, 1):

        @pl.when(interior[side])
        def _():
            n_copy(side).wait_send()


def on_device(directions, diag_blocks, left_blocks, right_blocks, param_blocks, obs_weight, end_junction):
    args = (directions, diag_blocks, left_blocks, right_blocks, param_blocks, obs_weight, jnp.swapaxes(end_junction, 1, 2))
    args = tuple(pltpu.with_memory_space_constraint(a, pltpu.HBM) for a in args)
    dma = pltpu.SemaphoreType.DMA

    def tiles(*counts):
        return pltpu.VMEM(counts + (PIPES, LANES), F32)

    return pl.pallas_call(
        kernel,
        out_shape=pltpu.VMEM(directions.shape, F32),
        in_specs=[pl.BlockSpec(memory_space=pl.ANY)] * len(args),
        out_specs=pl.BlockSpec(memory_space=pltpu.VMEM),
        scratch_shapes=[tiles(2, NPAR, COLS)]
        + [pltpu.VMEM(a.shape, a.dtype) for a in args[1:]]
        + [
            pltpu.VMEM((5 * NPAR * NPAR, PIPES, CELLS), F32),
            tiles(2, N_COEF),
            tiles(2, NPAR),
            tiles(2, COMP),
            tiles(2, COMP + 1),
            tiles(2, COMP + 1),
            pltpu.VMEM((Z_SIZE, 8, 24, LANES), F32),
            pltpu.VMEM((PIPES * J_W, 2 * LANES), F32),
            tiles(COMP),
            tiles(),
            tiles(2, COMP),
            tiles(2, COMP),
            dma((2,)),
            dma((6,)),
            dma((2,)),
            dma((2,)),
            dma,
            dma((8,)),
            dma,
            dma((8,)),
        ],
        compiler_params=pltpu.CompilerParams(
            collective_id=3, has_side_effects=True, vmem_limit_bytes=56 * 1024 * 1024
        ),
    )(*args)


def solution(mesh):
    return jax.shard_map(
        on_device,
        mesh=mesh,
        in_specs=(
            P(None, None, "region", "sub"),
            P(None, None, "region", "sub"),
            P(None, None, "region", "sub"),
            P(None, None, "region", "sub"),
            P(None, None, "region", "sub"),
            P(None, "region", "sub"),
            P(),
        ),
        out_specs=P(None, None, "region", "sub"),
        check_vma=False,
    )
```

```python
import jax
import jax.numpy as jnp
from jax import lax
from jax.experimental import pallas as pl
from jax.experimental.pallas import tpu as pltpu
from jax.sharding import PartitionSpec as P

MESH = pl.DeviceIdType.MESH
F32 = jnp.float32
BF16 = jnp.bfloat16
X_SIZE, Z_SIZE = 4, 8
COMP, NPAR, COLS, PIPES, CELLS = 4, 2, 64, 8, 256
LANES = 128
Z_STEPS = (4, 3, 5, 2, 6, 1, 7)
DIRECT = ((4, 0),)
PE, PN, DD, CIN, COUT, WT = 0, 8, 16, 32, 48, 64
N_COEF = 68
J_W, J_ID, J_SPAN = 24, 28, 32
ROWS = 18


def iota(shape, dim):
    return lax.broadcasted_iota(jnp.int32, shape, dim)


def split(v, kind=BF16):
    parts = []
    for _ in range(3):
        part = v.astype(BF16)
        v = v - part.astype(F32)
        parts.append(part.astype(kind))
    return parts


def spread(column):
    return jnp.broadcast_to(column, (PIPES, LANES))


def kernel(
    dir_in, diag_in, left_in, right_in, par_in, wt_in, ids_in, hess,
    dirs, diag, left, right, par, wt, ids,
    band, coef, comp, src_s, n_send, n_recv, jbuf, j_sum, j_weight, j_own, mean_s, mean_a,
    dir_sem, in_sem, ns_sem, nr_sem, zs_sem, zr_sem, ys_sem, yr_sem,
):
    g = lax.axis_index("region")
    s = lax.axis_index("sub")
    x, z = g // Z_SIZE, lax.rem(g, Z_SIZE)
    me = 2 * x + s // 7
    is_first, is_last = s == 0, s == 7
    is_end = jnp.logical_or(is_first, is_last)
    early = jnp.logical_and(is_end, z < Z_SIZE // 2)
    pe = s // 7

    z_peers = [(x * Z_SIZE + lax.rem(z + k, Z_SIZE), s) for k in Z_STEPS]

    def plane_peers(plane):
        xr = [lax.rem(x + k, X_SIZE) * Z_SIZE + plane for k in range(X_SIZE)]
        return [(xr[2], 7 - s), (xr[1], 7 - s), (xr[3], 7 - s), (xr[2], s), (xr[1], s), (xr[3], s), (xr[0], 7 - s)]

    y_peers = plane_peers(z)

    def to(peer):
        return dict(device_id={"region": peer[0], "sub": peer[1]}, device_id_type=MESH)

    interior = (s > 0, s < 7)
    beside = ((g, s - 1), (g, s + 1))

    def half_load(half):
        start = pl.multiple_of(half * LANES, LANES)
        return pltpu.make_async_copy(dir_in.at[:, :, :, pl.ds(start, LANES)], dirs.at[half], dir_sem.at[half])

    loads = [
        pltpu.make_async_copy(a, b, in_sem.at[i])
        for i, (a, b) in enumerate(
            ((par_in, par), (diag_in, diag), (wt_in, wt), (left_in, left), (right_in, right), (ids_in, ids))
        )
    ]
    half_load(pe).start()
    for load in loads:
        load.start()
    barrier = pltpu.get_barrier_semaphore()

    @pl.when(is_end)
    def _():
        for peer in z_peers + y_peers:
            pl.semaphore_signal(barrier, inc=1, **to(peer))
        for source, target in DIRECT:

            @pl.when(z == target)
            def _():
                for peer in plane_peers(source):
                    pl.semaphore_signal(barrier, inc=1, **to(peer))

    for side in (0, 1):

        @pl.when(interior[side])
        def _():
            pl.semaphore_signal(barrier, inc=1, **to(beside[side]))

    half_load(1 - pe).start()
    for load in loads:
        load.wait()

    lane = iota((PIPES, LANES), 1)
    even = lax.rem(lane, 2) == 0
    lane2 = iota((PIPES, CELLS), 1)
    quarter = lax.rem(iota((PIPES, LANES), 0), 4)
    zero = jnp.zeros((PIPES, LANES), F32)

    ends = jnp.logical_or(
        jnp.logical_and(lane2 == 0, is_first), jnp.logical_and(lane2 == CELLS - 1, is_last)
    )
    for c in range(COMP):
        diag[c, c] = diag[c, c] - jnp.where(ends, 0.5, 0.0)

    def swap(v):
        return jnp.where(even, pltpu.roll(v, LANES - 1, 1), pltpu.roll(v, 1, 1))

    def nxt(v):
        return pltpu.roll(v, LANES - 1, 1)

    def lane_pack(values):
        tile = zero
        for i, v in enumerate(values):
            tile = jnp.where(lane == i, v, tile)
        return tile

    def end_cells(side):
        parts = [[zero, zero] for _ in range(NPAR)]
        for r in range(COLS):
            here = lane // 2 == r
            for k in range(NPAR):
                moved = pltpu.roll(dirs[side, k, r], (2 * r + 2 * side) % LANES, 1)
                parts[k][r % 2] = jnp.where(here, moved, parts[k][r % 2])
        tiles = [a + b for a, b in parts]
        for k in range(NPAR):
            comp[side, k] = swap(tiles[k]) if side else tiles[k]

    def end_coefficients(side, outside):
        e, n = (CELLS - 1, CELLS - 2) if side else (0, 1)
        inner, outer = (left, right) if side else (right, left)
        for t in range(COMP):
            coef[side, WT + t] = spread(wt[t, :, e : e + 1])
            for k in range(NPAR):
                coef[side, PE + NPAR * t + k] = spread(par[t, k, :, e : e + 1])
                coef[side, PN + NPAR * t + k] = spread(par[t, k, :, n : n + 1])
            for q in range(COMP):
                coef[side, DD + COMP * t + q] = spread(diag[t, q, :, e : e + 1])
                coef[side, CIN + COMP * t + q] = spread(inner[t, q, :, e : e + 1])
                if outside:
                    coef[side, COUT + COMP * t + q] = spread(outer[t, q, :, e : e + 1])

    for side, chosen in ((0, is_first), (1, is_last)):

        @pl.when(chosen)
        def _():
            row = jnp.where(g >= 16, ids[side, :, LANES:], ids[side, :, :LANES]).astype(F32)
            mine = lane == PIPES * lax.rem(g, 16) + iota((PIPES, LANES), 0)
            own = spread(jnp.sum(jnp.where(mine, row, 0.0), axis=1, keepdims=True))
            span = slice(side * LANES, side * LANES + LANES)
            inner = left if side else right
            here = [[par[t, k, :, span] for k in range(NPAR)] for t in range(COMP)]
            beyond = [[pltpu.roll(v, 1 if side else LANES - 1, 1) for v in vs] for vs in here]
            weight = [wt[t, :, span] for t in range(COMP)]
            pack = [v for vs in here for v in vs]
            for near in (True, False):
                for t in range(COMP):
                    for k in range(NPAR):
                        total = here[t][k] if near else zero
                        for q in range(COMP):
                            block, cell = (diag, here) if near else (inner, beyond)
                            total = total + block[t, q, :, span] * cell[q][k]
                        pack.append(weight[t] * total)
            pack += weight
            tile = jnp.where(lane == J_ID, own, 0.0)
            for i, v in enumerate(pack):
                tile = jnp.where(lane == i, pltpu.roll(v, (i - (LANES - 1) * side) % LANES, 1), tile)
            half_load(pe).wait()
            end_cells(side)
            for k in range(NPAR):
                jbuf[z, me, 8 * k : 8 * k + 8] = comp[side, k]
            for m in range(1, 4):
                tile = jnp.where(quarter == m, pltpu.roll(tile, J_SPAN * m, 1), tile)
            for m in range(2):
                jbuf[z, me, 16 + m : 17 + m] = jnp.sum(tile[4 * m : 4 * m + 4], axis=0, keepdims=True)
            j_own[...] = own

    def n_copy(side):
        return pltpu.make_async_remote_copy(
            src_ref=n_send.at[side],
            dst_ref=n_recv.at[1 - side],
            send_sem=ns_sem.at[side],
            recv_sem=nr_sem.at[1 - side],
            **to(beside[side]),
        )

    def slot(plane):
        return jbuf.at[plane, me, pl.ds(0, ROWS)]

    def z_copy(plane, peer):
        return pltpu.make_async_remote_copy(
            src_ref=slot(plane), dst_ref=slot(plane), send_sem=zs_sem, recv_sem=zr_sem.at[plane], **to(peer)
        )

    def forward(plane, peers=y_peers):
        for peer in peers:
            pltpu.make_async_remote_copy(
                src_ref=slot(plane), dst_ref=slot(plane), send_sem=ys_sem, recv_sem=yr_sem.at[plane], **to(peer)
            ).start()

    def prepare():
        half_load(1 - pe).wait()

        @pl.when(jnp.logical_not(is_end))
        def _():
            half_load(pe).wait()

        for side in (0, 1):

            @pl.when(interior[side])
            def _():
                end_cells(side)
                end_coefficients(side, True)
                source = []
                for t in range(COMP):
                    total = zero
                    for k in range(NPAR):
                        factor = jnp.where(even, coef[side, PE + NPAR * t + k], coef[side, PN + NPAR * t + k])
                        total = total + factor * comp[side, k]
                    source.append(total)
                after = [nxt(v) for v in source]
                for t in range(COMP):
                    total = source[t]
                    for q in range(COMP):
                        total = total + coef[side, DD + COMP * t + q] * source[q]
                        total = total + coef[side, CIN + COMP * t + q] * after[q]
                    src_s[side, t] = source[t]
                    n_send[side, t] = jnp.where(even, source[t], pltpu.roll(coef[side, WT + t] * total, 1, 1))
                n_send[side, COMP] = lane_pack(
                    [coef[side, COUT + i] for i in range(COMP * COMP)] + [coef[side, WT + t] for t in range(COMP)]
                )

        for side, chosen in ((0, is_first), (1, is_last)):

            @pl.when(chosen)
            def _():
                end_coefficients(side, False)

    def piece():
        def up(v):
            return jnp.where(lane2 == CELLS - 1, 0.0, pltpu.roll(v, CELLS - 1, 1))

        def down(v):
            return jnp.where(lane2 == 0, 0.0, pltpu.roll(v, 1, 1))

        p_here = [[par[t, k] for k in range(NPAR)] for t in range(COMP)]
        p_up = [[up(v) for v in vs] for vs in p_here]
        p_down = [[down(v) for v in vs] for vs in p_here]

        def product(blocks, cells, start):
            rows = []
            for t in range(COMP):
                row = []
                for k in range(NPAR):
                    total = start[t][k] if start is not None else None
                    for q in range(COMP):
                        term = blocks[t, q] * cells[q][k]
                        total = term if total is None else total + term
                    row.append(total)
                rows.append(row)
            return rows

        b0 = product(diag, p_here, p_here)
        bm = product(left, p_down, None)
        bp = product(right, p_up, None)
        weight = [wt[t] for t in range(COMP)]
        u0 = [[weight[t] * v for v in b0[t]] for t in range(COMP)]
        um = [[weight[t] * v for v in bm[t]] for t in range(COMP)]
        upl = [[weight[t] * v for v in bp[t]] for t in range(COMP)]

        def inner_sum(a, b, k, q):
            total = a[0][k] * b[0][q]
            for t in range(1, COMP):
                total = total + a[t][k] * b[t][q]
            return total

        for k in range(NPAR):
            for q in range(NPAR):
                i = NPAR * k + q
                if k <= q:
                    centre = inner_sum(b0, u0, k, q) + down(inner_sum(bp, upl, k, q)) + up(inner_sum(bm, um, k, q))
                    band[8 + i] = centre
                    if k != q:
                        band[8 + NPAR * q + k] = centre
                one = inner_sum(b0, upl, k, q) + up(inner_sum(bm, u0, k, q))
                two = up(inner_sum(bm, upl, k, q))
                band[12 + i] = one
                band[16 + i] = two
                band[4 + NPAR * q + k] = down(one)
                band[NPAR * q + k] = down(down(two))

        def wide_step(r, carry):
            shifted = []
            for k in range(NPAR):
                a = dirs[0, k, r]
                b = dirs[1, k, r]
                per_offset = []
                for off in (-2, -1, 0, 1, 2):
                    if off == 0:
                        per_offset.append((a, b))
                        continue
                    ra = pltpu.roll(a, -off % LANES, 1)
                    rb = pltpu.roll(b, -off % LANES, 1)
                    if off < 0:
                        per_offset.append((ra, jnp.where(lane < -off, ra, rb)))
                    else:
                        per_offset.append((jnp.where(lane >= LANES - off, rb, ra), rb))
                shifted.append(per_offset)
            for half in (0, 1):
                span = slice(half * LANES, half * LANES + LANES)
                for k in range(NPAR):
                    total = None
                    for o in range(5):
                        for q in range(NPAR):
                            term = band[4 * o + NPAR * k + q, :, span] * shifted[q][o][half]
                            total = term if total is None else total + term
                    hess[k, r, :, span] = total
            return carry

        lax.fori_loop(0, COLS, wide_step, 0, unroll=4)

    @pl.when(early)
    def _():
        prepare()
        piece()

    expected = jnp.where(is_end, 1 + len(z_peers) + len(y_peers), 2)
    for source, _ in DIRECT:
        expected = expected + jnp.where(jnp.logical_and(is_end, z == source), len(y_peers), 0)
    pl.semaphore_wait(barrier, expected)

    @pl.when(is_end)
    def _():
        for plane in range(Z_SIZE):

            @pl.when(z != plane)
            def _():
                z_copy(z, (x * Z_SIZE + plane, s)).start()

            for source, target in DIRECT:
                if target == plane:

                    @pl.when(z == source)
                    def _():
                        forward(z, plane_peers(target))

        forward(z)

    @pl.when(jnp.logical_not(early))
    def _():
        prepare()

    for side in (0, 1):

        @pl.when(interior[side])
        def _():
            n_copy(side).start()

    @pl.when(jnp.logical_not(early))
    def _():
        piece()

    def finish(side):
        change = [coef[side, WT + t] * mean_s[side, t] for t in range(COMP)]
        at_end, at_next = [], []
        for q in range(COMP):
            total = change[q] + mean_a[side, q]
            other = zero
            for t in range(COMP):
                total = total + coef[side, DD + COMP * t + q] * change[t]
                other = other + coef[side, CIN + COMP * t + q] * change[t]
            at_end.append(total)
            at_next.append(other)
        corr = []
        for k in range(NPAR):
            c0, c1 = zero, zero
            for t in range(COMP):
                c0 = c0 + coef[side, PE + NPAR * t + k] * at_end[t]
                c1 = c1 + coef[side, PN + NPAR * t + k] * at_next[t]
            straight = jnp.where(even, c0, pltpu.roll(c1, 1, 1))
            corr.append(swap(straight) if side else straight)
        edge = LANES - 2 if side else 0
        here = jnp.logical_and(lane >= edge, lane < edge + 2)
        span = slice(side * LANES, side * LANES + LANES)
        for r in range(COLS):
            for k in range(NPAR):
                moved = pltpu.roll(corr[k], (LANES + edge - 2 * r) % LANES, 1)
                hess[k, r, :, span] = hess[k, r, :, span] + jnp.where(here, moved, 0.0)

    @pl.when(is_end)
    def _():
        for k in reversed(Z_STEPS):
            plane = lax.rem(z + Z_SIZE - k, Z_SIZE)
            z_copy(plane, z_peers[0]).wait_recv()
            sent = z < 0
            for source, target in DIRECT:
                sent = jnp.logical_or(sent, jnp.logical_and(z == target, plane == source))

            @pl.when(jnp.logical_not(sent))
            def _():
                forward(plane)


    for side in (0, 1):

        @pl.when(interior[side])
        def _():
            n_copy(1 - side).wait_recv()
            theirs = n_recv[side, COMP]
            out_block = [spread(theirs[:, i : i + 1]) for i in range(COMP * COMP)]
            out_weight = [spread(theirs[:, COMP * COMP + t : COMP * COMP + t + 1]) for t in range(COMP)]
            pairs = [n_recv[side, t] for t in range(COMP)]
            adjoint = []
            for t in range(COMP):
                total, change = zero, zero
                for q in range(COMP):
                    total = total + out_block[COMP * t + q] * src_s[side, q]
                    change = change + coef[side, COUT + COMP * t + q] * pairs[q]
                adjoint.append(nxt(pairs[t]) + out_weight[t] * total)
                mean_s[side, t] = change
            for q in range(COMP):
                total = zero
                for t in range(COMP):
                    total = total + out_block[COMP * t + q] * adjoint[t]
                mean_a[side, q] = total
            finish(side)

    @pl.when(is_end)
    def _():
        own = j_own[...]
        rows = 8 * PIPES

        def arrivals(planes, sem):
            span = jbuf.at[planes, pl.ds(0, 7), pl.ds(0, ROWS)]
            return pltpu.make_async_remote_copy(
                src_ref=span, dst_ref=span, send_sem=ys_sem, recv_sem=yr_sem.at[sem], **to(y_peers[0])
            )

        j_sum[...] = jnp.zeros_like(j_sum)
        j_weight[...] = jnp.zeros_like(j_weight)
        degree = zero
        for end in (0, 1):
            for half in (0, 1):
                row = ids[end, :, half * LANES : half * LANES + LANES].astype(F32)
                degree = degree + jnp.where(row == own, 1.0, 0.0)
        share = 1.0 / spread(jnp.sum(degree, axis=1, keepdims=True))

        def add_planes(j, carry):
            pair = [lax.rem(z + Z_SIZE - j, Z_SIZE), lax.rem(z + 1 + j, Z_SIZE)]
            columns, tiles = [], []
            for plane in pair:
                arrivals(plane, plane).wait_recv()
                columns.append([jbuf[plane, :, 8 * k : 8 * k + 8].reshape(rows, LANES) for k in range(NPAR)])
                for q in range(8):
                    packed = jnp.where(
                        iota((PIPES, LANES), 0) < 4, jbuf[plane, q, 16:17], jbuf[plane, q, 17:18]
                    )
                    tile = packed
                    for m in range(1, 4):
                        tile = jnp.where(quarter == m, pltpu.roll(packed, LANES - J_SPAN * m, 1), tile)
                    tiles.append(tile)
            x_parts = split(jnp.concatenate([jnp.concatenate(c, axis=1) for c in columns]))
            coefs = jnp.concatenate(tiles).T
            same = coefs[J_ID : J_ID + 1] == own[:, 0:1]
            w_parts = [
                jnp.concatenate([jnp.where(same, v[i : i + 1], 0.0) for i in range(J_W)]).astype(BF16)
                for v in split(coefs[:J_SPAN], F32)
            ]
            order = ((0, 0), (0, 1), (1, 0), (0, 2), (2, 0), (1, 1))
            j_sum[...] += jnp.dot(
                jnp.concatenate([w_parts[i] for i, _ in order], axis=1),
                jnp.concatenate([x_parts[i] for _, i in order]),
                preferred_element_type=F32,
            )
            for t in range(COMP):
                j_weight[t] += jnp.where(same, coefs[J_W + t : J_W + t + 1], 0.0)
            return carry

        lax.fori_loop(0, Z_SIZE // 2, add_planes, 0)

        def part(c, k):
            return j_sum[PIPES * c : PIPES * c + PIPES, LANES * k : LANES * k + LANES]

        for t in range(COMP):
            c = NPAR * t
            mean = share * (part(c, 0) + part(c + 1, 1))
            near = part(8 + c, 0) + part(9 + c, 1)
            far = part(16 + c, 0) + part(17 + c, 1)
            weights = spread(jnp.sum(j_weight[t], axis=1, keepdims=True))
            mean_s[pe, t] = 0.5 * mean
            mean_a[pe, t] = 0.5 * share * (near + nxt(far) + 0.5 * weights * mean)
        for side, chosen in ((0, is_first), (1, is_last)):

            @pl.when(chosen)
            def _():
                finish(side)

        for plane in range(Z_SIZE):
            sent = z < 0
            for source, target in DIRECT:
                if source == plane:
                    sent = jnp.logical_or(sent, z == target)

            @pl.when(jnp.logical_not(sent))
            def _():
                arrivals(plane, plane).wait_send()

        for source, target in DIRECT:

            @pl.when(z == source)
            def _():
                arrivals(target, target).wait_send()

        span = jbuf.at[0, pl.ds(0, 7), pl.ds(0, ROWS)]
        pltpu.make_async_remote_copy(
            src_ref=span, dst_ref=span, send_sem=zs_sem, recv_sem=yr_sem.at[0], **to(z_peers[0])
        ).wait_send()

    for side in (0, 1):

        @pl.when(interior[side])
        def _():
            n_copy(side).wait_send()


def on_device(directions, diag_blocks, left_blocks, right_blocks, param_blocks, obs_weight, end_junction):
    args = (directions, diag_blocks, left_blocks, right_blocks, param_blocks, obs_weight, jnp.swapaxes(end_junction, 1, 2))
    args = tuple(pltpu.with_memory_space_constraint(a, pltpu.HBM) for a in args)
    dma = pltpu.SemaphoreType.DMA

    def tiles(*counts):
        return pltpu.VMEM(counts + (PIPES, LANES), F32)

    return pl.pallas_call(
        kernel,
        out_shape=pltpu.VMEM(directions.shape, F32),
        in_specs=[pl.BlockSpec(memory_space=pl.ANY)] * len(args),
        out_specs=pl.BlockSpec(memory_space=pltpu.VMEM),
        scratch_shapes=[tiles(2, NPAR, COLS)]
        + [pltpu.VMEM(a.shape, a.dtype) for a in args[1:]]
        + [
            pltpu.VMEM((5 * NPAR * NPAR, PIPES, CELLS), F32),
            tiles(2, N_COEF),
            tiles(2, NPAR),
            tiles(2, COMP),
            tiles(2, COMP + 1),
            tiles(2, COMP + 1),
            pltpu.VMEM((Z_SIZE, 8, 24, LANES), F32),
            pltpu.VMEM((PIPES * J_W, 2 * LANES), F32),
            tiles(COMP),
            tiles(),
            tiles(2, COMP),
            tiles(2, COMP),
            dma((2,)),
            dma((6,)),
            dma((2,)),
            dma((2,)),
            dma,
            dma((8,)),
            dma,
            dma((8,)),
        ],
        compiler_params=pltpu.CompilerParams(
            collective_id=3, has_side_effects=True, vmem_limit_bytes=56 * 1024 * 1024
        ),
    )(*args)


def solution(mesh):
    return jax.shard_map(
        on_device,
        mesh=mesh,
        in_specs=(
            P(None, None, "region", "sub"),
            P(None, None, "region", "sub"),
            P(None, None, "region", "sub"),
            P(None, None, "region", "sub"),
            P(None, None, "region", "sub"),
            P(None, "region", "sub"),
            P(),
        ),
        out_specs=P(None, None, "region", "sub"),
        check_vma=False,
    )
```

```python
import jax
import jax.numpy as jnp
from jax import lax
from jax.experimental import pallas as pl
from jax.experimental.pallas import tpu as pltpu
from jax.sharding import PartitionSpec as P

MESH = pl.DeviceIdType.MESH
F32 = jnp.float32
BF16 = jnp.bfloat16
X_SIZE, Z_SIZE = 4, 8
COMP, NPAR, COLS, PIPES, CELLS = 4, 2, 64, 8, 256
LANES = 128
Z_STEPS = (4, 3, 5, 2, 6, 1, 7)
DIRECT = ((4, 0),)
PE, PN, DD, CIN, COUT, WT = 0, 8, 16, 32, 48, 64
N_COEF = 68
J_W, J_ID, J_SPAN = 24, 28, 32
ROWS = 18


def iota(shape, dim):
    return lax.broadcasted_iota(jnp.int32, shape, dim)


def split(v, kind=BF16):
    parts = []
    for _ in range(3):
        part = v.astype(BF16)
        v = v - part.astype(F32)
        parts.append(part.astype(kind))
    return parts


def spread(column):
    return jnp.broadcast_to(column, (PIPES, LANES))


def kernel(
    dir_in, diag_in, left_in, right_in, par_in, wt_in, ids_in, hess, last,
    dirs, diag, left, right, par, wt, ids,
    band, coef, comp, src_s, n_send, n_recv, jbuf, j_sum, j_weight, j_own, mean_s, mean_a,
    dir_sem, in_sem, ns_sem, nr_sem, zs_sem, zr_sem, ys_sem, yr_sem,
):
    g = lax.axis_index("region")
    s = lax.axis_index("sub")
    x, z = g // Z_SIZE, lax.rem(g, Z_SIZE)
    me = 2 * x + s // 7
    is_first, is_last = s == 0, s == 7
    is_end = jnp.logical_or(is_first, is_last)
    early = jnp.logical_and(is_end, z < Z_SIZE // 2)
    pe = s // 7

    z_peers = [(x * Z_SIZE + lax.rem(z + k, Z_SIZE), s) for k in Z_STEPS]

    def plane_peers(plane):
        xr = [lax.rem(x + k, X_SIZE) * Z_SIZE + plane for k in range(X_SIZE)]
        return [(xr[2], 7 - s), (xr[1], 7 - s), (xr[3], 7 - s), (xr[2], s), (xr[1], s), (xr[3], s), (xr[0], 7 - s)]

    y_peers = plane_peers(z)

    def to(peer):
        return dict(device_id={"region": peer[0], "sub": peer[1]}, device_id_type=MESH)

    interior = (s > 0, s < 7)
    beside = ((g, s - 1), (g, s + 1))

    def half_load(half):
        start = pl.multiple_of(half * LANES, LANES)
        return pltpu.make_async_copy(dir_in.at[:, :, :, pl.ds(start, LANES)], dirs.at[half], dir_sem.at[half])

    loads = [
        pltpu.make_async_copy(a, b, in_sem.at[i])
        for i, (a, b) in enumerate(
            ((par_in, par), (diag_in, diag), (wt_in, wt), (left_in, left), (right_in, right), (ids_in, ids))
        )
    ]
    half_load(pe).start()
    for load in loads:
        load.start()
    barrier = pltpu.get_barrier_semaphore()

    @pl.when(is_end)
    def _():
        for peer in z_peers + y_peers:
            pl.semaphore_signal(barrier, inc=1, **to(peer))
        for source, target in DIRECT:

            @pl.when(z == target)
            def _():
                for peer in plane_peers(source):
                    pl.semaphore_signal(barrier, inc=1, **to(peer))

    for side in (0, 1):

        @pl.when(interior[side])
        def _():
            pl.semaphore_signal(barrier, inc=1, **to(beside[side]))

    half_load(1 - pe).start()
    for load in loads:
        load.wait()

    lane = iota((PIPES, LANES), 1)
    even = lax.rem(lane, 2) == 0
    lane2 = iota((PIPES, CELLS), 1)
    quarter = lax.rem(iota((PIPES, LANES), 0), 4)
    zero = jnp.zeros((PIPES, LANES), F32)

    ends = jnp.logical_or(
        jnp.logical_and(lane2 == 0, is_first), jnp.logical_and(lane2 == CELLS - 1, is_last)
    )
    for c in range(COMP):
        diag[c, c] = diag[c, c] - jnp.where(ends, 0.5, 0.0)

    def swap(v):
        return jnp.where(even, pltpu.roll(v, LANES - 1, 1), pltpu.roll(v, 1, 1))

    def nxt(v):
        return pltpu.roll(v, LANES - 1, 1)

    def lane_pack(values):
        tile = zero
        for i, v in enumerate(values):
            tile = jnp.where(lane == i, v, tile)
        return tile

    def end_cells(side):
        parts = [[zero, zero] for _ in range(NPAR)]
        for r in range(COLS):
            here = lane // 2 == r
            for k in range(NPAR):
                moved = pltpu.roll(dirs[side, k, r], (2 * r + 2 * side) % LANES, 1)
                parts[k][r % 2] = jnp.where(here, moved, parts[k][r % 2])
        tiles = [a + b for a, b in parts]
        for k in range(NPAR):
            comp[side, k] = swap(tiles[k]) if side else tiles[k]

    def end_coefficients(side, outside):
        e, n = (CELLS - 1, CELLS - 2) if side else (0, 1)
        inner, outer = (left, right) if side else (right, left)
        for t in range(COMP):
            coef[side, WT + t] = spread(wt[t, :, e : e + 1])
            for k in range(NPAR):
                coef[side, PE + NPAR * t + k] = spread(par[t, k, :, e : e + 1])
                coef[side, PN + NPAR * t + k] = spread(par[t, k, :, n : n + 1])
            for q in range(COMP):
                coef[side, DD + COMP * t + q] = spread(diag[t, q, :, e : e + 1])
                coef[side, CIN + COMP * t + q] = spread(inner[t, q, :, e : e + 1])
                if outside:
                    coef[side, COUT + COMP * t + q] = spread(outer[t, q, :, e : e + 1])

    for side, chosen in ((0, is_first), (1, is_last)):

        @pl.when(chosen)
        def _():
            row = jnp.where(g >= 16, ids[side, :, LANES:], ids[side, :, :LANES]).astype(F32)
            mine = lane == PIPES * lax.rem(g, 16) + iota((PIPES, LANES), 0)
            own = spread(jnp.sum(jnp.where(mine, row, 0.0), axis=1, keepdims=True))
            span = slice(side * LANES, side * LANES + LANES)
            inner = left if side else right
            here = [[par[t, k, :, span] for k in range(NPAR)] for t in range(COMP)]
            beyond = [[pltpu.roll(v, 1 if side else LANES - 1, 1) for v in vs] for vs in here]
            weight = [wt[t, :, span] for t in range(COMP)]
            pack = [v for vs in here for v in vs]
            for near in (True, False):
                for t in range(COMP):
                    for k in range(NPAR):
                        total = here[t][k] if near else zero
                        for q in range(COMP):
                            block, cell = (diag, here) if near else (inner, beyond)
                            total = total + block[t, q, :, span] * cell[q][k]
                        pack.append(weight[t] * total)
            pack += weight
            tile = jnp.where(lane == J_ID, own, 0.0)
            for i, v in enumerate(pack):
                tile = jnp.where(lane == i, pltpu.roll(v, (i - (LANES - 1) * side) % LANES, 1), tile)
            half_load(pe).wait()
            end_cells(side)
            for k in range(NPAR):
                jbuf[z, me, 8 * k : 8 * k + 8] = comp[side, k]
            for m in range(1, 4):
                tile = jnp.where(quarter == m, pltpu.roll(tile, J_SPAN * m, 1), tile)
            for m in range(2):
                jbuf[z, me, 16 + m : 17 + m] = jnp.sum(tile[4 * m : 4 * m + 4], axis=0, keepdims=True)
            j_own[...] = own

    def n_copy(side):
        return pltpu.make_async_remote_copy(
            src_ref=n_send.at[side],
            dst_ref=n_recv.at[1 - side],
            send_sem=ns_sem.at[side],
            recv_sem=nr_sem.at[1 - side],
            **to(beside[side]),
        )

    def slot(plane):
        return jbuf.at[plane, me, pl.ds(0, ROWS)]

    def z_copy(plane, peer):
        return pltpu.make_async_remote_copy(
            src_ref=slot(plane), dst_ref=slot(plane), send_sem=zs_sem, recv_sem=zr_sem.at[plane], **to(peer)
        )

    def forward(plane, peers=y_peers):
        for peer in peers:
            pltpu.make_async_remote_copy(
                src_ref=slot(plane), dst_ref=slot(plane), send_sem=ys_sem, recv_sem=yr_sem.at[plane], **to(peer)
            ).start()

    def prepare():
        half_load(1 - pe).wait()

        @pl.when(jnp.logical_not(is_end))
        def _():
            half_load(pe).wait()

        for side in (0, 1):

            @pl.when(interior[side])
            def _():
                end_cells(side)
                end_coefficients(side, True)
                source = []
                for t in range(COMP):
                    total = zero
                    for k in range(NPAR):
                        factor = jnp.where(even, coef[side, PE + NPAR * t + k], coef[side, PN + NPAR * t + k])
                        total = total + factor * comp[side, k]
                    source.append(total)
                after = [nxt(v) for v in source]
                for t in range(COMP):
                    total = source[t]
                    for q in range(COMP):
                        total = total + coef[side, DD + COMP * t + q] * source[q]
                        total = total + coef[side, CIN + COMP * t + q] * after[q]
                    src_s[side, t] = source[t]
                    n_send[side, t] = jnp.where(even, source[t], pltpu.roll(coef[side, WT + t] * total, 1, 1))
                n_send[side, COMP] = lane_pack(
                    [coef[side, COUT + i] for i in range(COMP * COMP)] + [coef[side, WT + t] for t in range(COMP)]
                )

        for side, chosen in ((0, is_first), (1, is_last)):

            @pl.when(chosen)
            def _():
                end_coefficients(side, False)

    def piece():
        def up(v):
            return jnp.where(lane2 == CELLS - 1, 0.0, pltpu.roll(v, CELLS - 1, 1))

        def down(v):
            return jnp.where(lane2 == 0, 0.0, pltpu.roll(v, 1, 1))

        p_here = [[par[t, k] for k in range(NPAR)] for t in range(COMP)]
        p_up = [[up(v) for v in vs] for vs in p_here]
        p_down = [[down(v) for v in vs] for vs in p_here]

        def product(blocks, cells, start):
            rows = []
            for t in range(COMP):
                row = []
                for k in range(NPAR):
                    total = start[t][k] if start is not None else None
                    for q in range(COMP):
                        term = blocks[t, q] * cells[q][k]
                        total = term if total is None else total + term
                    row.append(total)
                rows.append(row)
            return rows

        b0 = product(diag, p_here, p_here)
        bm = product(left, p_down, None)
        bp = product(right, p_up, None)
        weight = [wt[t] for t in range(COMP)]
        u0 = [[weight[t] * v for v in b0[t]] for t in range(COMP)]
        um = [[weight[t] * v for v in bm[t]] for t in range(COMP)]
        upl = [[weight[t] * v for v in bp[t]] for t in range(COMP)]

        def inner_sum(a, b, k, q):
            total = a[0][k] * b[0][q]
            for t in range(1, COMP):
                total = total + a[t][k] * b[t][q]
            return total

        for k in range(NPAR):
            for q in range(NPAR):
                i = NPAR * k + q
                if k <= q:
                    centre = inner_sum(b0, u0, k, q) + down(inner_sum(bp, upl, k, q)) + up(inner_sum(bm, um, k, q))
                    band[8 + i] = centre
                    if k != q:
                        band[8 + NPAR * q + k] = centre
                one = inner_sum(b0, upl, k, q) + up(inner_sum(bm, u0, k, q))
                two = up(inner_sum(bm, upl, k, q))
                band[12 + i] = one
                band[16 + i] = two
                band[4 + NPAR * q + k] = down(one)
                band[NPAR * q + k] = down(down(two))

        def wide_step(r, carry):
            shifted = []
            for k in range(NPAR):
                a = dirs[0, k, r]
                b = dirs[1, k, r]
                per_offset = []
                for off in (-2, -1, 0, 1, 2):
                    if off == 0:
                        per_offset.append((a, b))
                        continue
                    ra = pltpu.roll(a, -off % LANES, 1)
                    rb = pltpu.roll(b, -off % LANES, 1)
                    if off < 0:
                        per_offset.append((ra, jnp.where(lane < -off, ra, rb)))
                    else:
                        per_offset.append((jnp.where(lane >= LANES - off, rb, ra), rb))
                shifted.append(per_offset)
            for half in (0, 1):
                span = slice(half * LANES, half * LANES + LANES)
                for k in range(NPAR):
                    total = None
                    for o in range(5):
                        for q in range(NPAR):
                            term = band[4 * o + NPAR * k + q, :, span] * shifted[q][o][half]
                            total = term if total is None else total + term
                    hess[k, r, :, span] = total
            return carry

        lax.fori_loop(0, COLS, wide_step, 0, unroll=4)

    @pl.when(early)
    def _():
        prepare()
        piece()

    expected = jnp.where(is_end, 1 + len(z_peers) + len(y_peers), 2)
    for source, _ in DIRECT:
        expected = expected + jnp.where(jnp.logical_and(is_end, z == source), len(y_peers), 0)
    pl.semaphore_wait(barrier, expected)

    @pl.when(is_end)
    def _():
        for plane in range(Z_SIZE):

            @pl.when(z != plane)
            def _():
                z_copy(z, (x * Z_SIZE + plane, s)).start()

            for source, target in DIRECT:
                if target == plane:

                    @pl.when(z == source)
                    def _():
                        forward(z, plane_peers(target))

        forward(z)

    @pl.when(jnp.logical_not(early))
    def _():
        prepare()

    for side in (0, 1):

        @pl.when(interior[side])
        def _():
            n_copy(side).start()

    @pl.when(jnp.logical_not(early))
    def _():
        piece()

    def finish(side):
        change = [coef[side, WT + t] * mean_s[side, t] for t in range(COMP)]
        at_end, at_next = [], []
        for q in range(COMP):
            total = change[q] + mean_a[side, q]
            other = zero
            for t in range(COMP):
                total = total + coef[side, DD + COMP * t + q] * change[t]
                other = other + coef[side, CIN + COMP * t + q] * change[t]
            at_end.append(total)
            at_next.append(other)
        corr = []
        for k in range(NPAR):
            c0, c1 = zero, zero
            for t in range(COMP):
                c0 = c0 + coef[side, PE + NPAR * t + k] * at_end[t]
                c1 = c1 + coef[side, PN + NPAR * t + k] * at_next[t]
            straight = jnp.where(even, c0, pltpu.roll(c1, 1, 1))
            corr.append(swap(straight) if side else straight)
        return corr

    def add_to_piece(side, corr):
        edge = LANES - 2 if side else 0
        here = jnp.logical_and(lane >= edge, lane < edge + 2)
        span = slice(side * LANES, side * LANES + LANES)
        for r in range(COLS):
            for k in range(NPAR):
                moved = pltpu.roll(corr[k], (LANES + edge - 2 * r) % LANES, 1)
                hess[k, r, :, span] = hess[k, r, :, span] + jnp.where(here, moved, 0.0)

    @pl.when(is_end)
    def _():
        for k in reversed(Z_STEPS):
            plane = lax.rem(z + Z_SIZE - k, Z_SIZE)
            z_copy(plane, z_peers[0]).wait_recv()
            sent = z < 0
            for source, target in DIRECT:
                sent = jnp.logical_or(sent, jnp.logical_and(z == target, plane == source))

            @pl.when(jnp.logical_not(sent))
            def _():
                forward(plane)


    for side in (0, 1):

        @pl.when(interior[side])
        def _():
            n_copy(1 - side).wait_recv()
            theirs = n_recv[side, COMP]
            out_block = [spread(theirs[:, i : i + 1]) for i in range(COMP * COMP)]
            out_weight = [spread(theirs[:, COMP * COMP + t : COMP * COMP + t + 1]) for t in range(COMP)]
            pairs = [n_recv[side, t] for t in range(COMP)]
            adjoint = []
            for t in range(COMP):
                total, change = zero, zero
                for q in range(COMP):
                    total = total + out_block[COMP * t + q] * src_s[side, q]
                    change = change + coef[side, COUT + COMP * t + q] * pairs[q]
                adjoint.append(nxt(pairs[t]) + out_weight[t] * total)
                mean_s[side, t] = change
            for q in range(COMP):
                total = zero
                for t in range(COMP):
                    total = total + out_block[COMP * t + q] * adjoint[t]
                mean_a[side, q] = total
            add_to_piece(side, finish(side))

    @pl.when(is_end)
    def _():
        own = j_own[...]
        rows = 8 * PIPES

        def arrivals(planes, sem):
            span = jbuf.at[planes, pl.ds(0, 7), pl.ds(0, ROWS)]
            return pltpu.make_async_remote_copy(
                src_ref=span, dst_ref=span, send_sem=ys_sem, recv_sem=yr_sem.at[sem], **to(y_peers[0])
            )

        j_sum[...] = jnp.zeros_like(j_sum)
        j_weight[...] = jnp.zeros_like(j_weight)
        degree = zero
        for end in (0, 1):
            for half in (0, 1):
                row = ids[end, :, half * LANES : half * LANES + LANES].astype(F32)
                degree = degree + jnp.where(row == own, 1.0, 0.0)
        share = 1.0 / spread(jnp.sum(degree, axis=1, keepdims=True))

        def add_planes(j, carry):
            pair = [lax.rem(z + Z_SIZE - j, Z_SIZE), lax.rem(z + 1 + j, Z_SIZE)]
            columns, tiles = [], []
            for plane in pair:
                arrivals(plane, plane).wait_recv()
                columns.append([jbuf[plane, :, 8 * k : 8 * k + 8].reshape(rows, LANES) for k in range(NPAR)])
                for q in range(8):
                    packed = jnp.where(
                        iota((PIPES, LANES), 0) < 4, jbuf[plane, q, 16:17], jbuf[plane, q, 17:18]
                    )
                    tile = packed
                    for m in range(1, 4):
                        tile = jnp.where(quarter == m, pltpu.roll(packed, LANES - J_SPAN * m, 1), tile)
                    tiles.append(tile)
            x_parts = split(jnp.concatenate([jnp.concatenate(c, axis=1) for c in columns]))
            coefs = jnp.concatenate(tiles).T
            same = coefs[J_ID : J_ID + 1] == own[:, 0:1]
            w_parts = [
                jnp.concatenate([jnp.where(same, v[i : i + 1], 0.0) for i in range(J_W)]).astype(BF16)
                for v in split(coefs[:J_SPAN], F32)
            ]
            order = ((0, 0), (0, 1), (1, 0), (0, 2), (2, 0), (1, 1))
            j_sum[...] += jnp.dot(
                jnp.concatenate([w_parts[i] for i, _ in order], axis=1),
                jnp.concatenate([x_parts[i] for _, i in order]),
                preferred_element_type=F32,
            )
            for t in range(COMP):
                j_weight[t] += jnp.where(same, coefs[J_W + t : J_W + t + 1], 0.0)
            return carry

        lax.fori_loop(0, Z_SIZE // 2, add_planes, 0)

        def part(c, k):
            return j_sum[PIPES * c : PIPES * c + PIPES, LANES * k : LANES * k + LANES]

        for t in range(COMP):
            c = NPAR * t
            mean = share * (part(c, 0) + part(c + 1, 1))
            near = part(8 + c, 0) + part(9 + c, 1)
            far = part(16 + c, 0) + part(17 + c, 1)
            weights = spread(jnp.sum(j_weight[t], axis=1, keepdims=True))
            mean_s[pe, t] = 0.5 * mean
            mean_a[pe, t] = 0.5 * share * (near + nxt(far) + 0.5 * weights * mean)
        for side, chosen in ((0, is_first), (1, is_last)):

            @pl.when(chosen)
            def _():
                for k, v in enumerate(finish(side)):
                    last[k] = v

        for plane in range(Z_SIZE):
            sent = z < 0
            for source, target in DIRECT:
                if source == plane:
                    sent = jnp.logical_or(sent, z == target)

            @pl.when(jnp.logical_not(sent))
            def _():
                arrivals(plane, plane).wait_send()

        for source, target in DIRECT:

            @pl.when(z == source)
            def _():
                arrivals(target, target).wait_send()

        span = jbuf.at[0, pl.ds(0, 7), pl.ds(0, ROWS)]
        pltpu.make_async_remote_copy(
            src_ref=span, dst_ref=span, send_sem=zs_sem, recv_sem=yr_sem.at[0], **to(z_peers[0])
        ).wait_send()

    for side in (0, 1):

        @pl.when(interior[side])
        def _():
            n_copy(side).wait_send()


def write_kernel(hess, last, out, piece, sem):
    s = lax.axis_index("sub")
    lane = iota((PIPES, LANES), 1)

    def write(side, k, source):
        span = pl.ds(side * LANES, LANES)
        return pltpu.make_async_copy(source, out.at[k, :, :, span], sem.at[side, k])

    for side in (0, 1):

        @pl.when(s != 7 * side)
        def _():
            for k in range(NPAR):
                write(side, k, hess.at[k, :, :, pl.ds(side * LANES, LANES)]).start()

    for side in (0, 1):

        @pl.when(s == 7 * side)
        def _():
            edge = LANES - 2 if side else 0
            here = jnp.logical_and(lane >= edge, lane < edge + 2)
            for k in range(NPAR):
                corr = last[k]
                for r in range(COLS):
                    moved = pltpu.roll(corr, (LANES + edge - 2 * r) % LANES, 1)
                    piece[k, r] = hess[k, r, :, side * LANES : side * LANES + LANES] + jnp.where(here, moved, 0.0)
                write(side, k, piece.at[k]).start()

    for side in (0, 1):
        for k in range(NPAR):
            write(side, k, piece.at[k]).wait()


def on_device(directions, diag_blocks, left_blocks, right_blocks, param_blocks, obs_weight, end_junction):
    args = (directions, diag_blocks, left_blocks, right_blocks, param_blocks, obs_weight, jnp.swapaxes(end_junction, 1, 2))
    args = tuple(pltpu.with_memory_space_constraint(a, pltpu.HBM) for a in args)
    dma = pltpu.SemaphoreType.DMA

    def tiles(*counts):
        return pltpu.VMEM(counts + (PIPES, LANES), F32)

    hess, last = pl.pallas_call(
        kernel,
        out_shape=(pltpu.VMEM(directions.shape, F32), tiles(NPAR)),
        in_specs=[pl.BlockSpec(memory_space=pl.ANY)] * len(args),
        out_specs=[pl.BlockSpec(memory_space=pltpu.VMEM)] * 2,
        scratch_shapes=[tiles(2, NPAR, COLS)]
        + [pltpu.VMEM(a.shape, a.dtype) for a in args[1:]]
        + [
            pltpu.VMEM((5 * NPAR * NPAR, PIPES, CELLS), F32),
            tiles(2, N_COEF),
            tiles(2, NPAR),
            tiles(2, COMP),
            tiles(2, COMP + 1),
            tiles(2, COMP + 1),
            pltpu.VMEM((Z_SIZE, 8, 24, LANES), F32),
            pltpu.VMEM((PIPES * J_W, 2 * LANES), F32),
            tiles(COMP),
            tiles(),
            tiles(2, COMP),
            tiles(2, COMP),
            dma((2,)),
            dma((6,)),
            dma((2,)),
            dma((2,)),
            dma,
            dma((8,)),
            dma,
            dma((8,)),
        ],
        compiler_params=pltpu.CompilerParams(
            collective_id=3, has_side_effects=True, vmem_limit_bytes=56 * 1024 * 1024
        ),
    )(*args)
    return pl.pallas_call(
        write_kernel,
        out_shape=jax.ShapeDtypeStruct(directions.shape, F32),
        in_specs=[pl.BlockSpec(memory_space=pltpu.VMEM)] * 2,
        out_specs=pl.BlockSpec(memory_space=pl.ANY),
        scratch_shapes=[tiles(NPAR, COLS), dma((2, NPAR))],
    )(*(pltpu.with_memory_space_constraint(v, pltpu.VMEM) for v in (hess, last)))


def solution(mesh):
    return jax.shard_map(
        on_device,
        mesh=mesh,
        in_specs=(
            P(None, None, "region", "sub"),
            P(None, None, "region", "sub"),
            P(None, None, "region", "sub"),
            P(None, None, "region", "sub"),
            P(None, None, "region", "sub"),
            P(None, "region", "sub"),
            P(),
        ),
        out_specs=P(None, None, "region", "sub"),
        check_vma=False,
    )
```

```python
import jax
import jax.numpy as jnp
from jax import lax
from jax.experimental import pallas as pl
from jax.experimental.pallas import tpu as pltpu
from jax.sharding import PartitionSpec as P

MESH = pl.DeviceIdType.MESH
F32 = jnp.float32
BF16 = jnp.bfloat16
X_SIZE, Z_SIZE = 4, 8
COMP, NPAR, COLS, PIPES, CELLS = 4, 2, 64, 8, 256
LANES = 128
Z_STEPS = (4, 3, 5, 2, 6, 1, 7)
DIRECT = ((4, 0),)
PE, PN, DD, CIN, COUT, WT = 0, 8, 16, 32, 48, 64
N_COEF = 68
J_W, J_ID, J_SPAN = 24, 28, 32
ROWS = 18


def iota(shape, dim):
    return lax.broadcasted_iota(jnp.int32, shape, dim)


def split(v, kind=BF16):
    parts = []
    for _ in range(3):
        part = v.astype(BF16)
        v = v - part.astype(F32)
        parts.append(part.astype(kind))
    return parts


def spread(column):
    return jnp.broadcast_to(column, (PIPES, LANES))


def kernel(
    dir_in, diag_in, left_in, right_in, par_in, wt_in, ids_in, hess, last,
    dirs, diag, left, right, par, wt, ids,
    band, coef, comp, src_s, n_send, n_recv, jbuf, j_sum, j_weight, j_own, mean_s, mean_a,
    dir_sem, in_sem, ns_sem, nr_sem, zs_sem, zr_sem, ys_sem, yr_sem,
):
    g = lax.axis_index("region")
    s = lax.axis_index("sub")
    x, z = g // Z_SIZE, lax.rem(g, Z_SIZE)
    me = 2 * x + s // 7
    is_first, is_last = s == 0, s == 7
    is_end = jnp.logical_or(is_first, is_last)
    early = jnp.logical_and(is_end, z < Z_SIZE // 2)
    pe = s // 7

    z_peers = [(x * Z_SIZE + lax.rem(z + k, Z_SIZE), s) for k in Z_STEPS]

    def plane_peers(plane):
        xr = [lax.rem(x + k, X_SIZE) * Z_SIZE + plane for k in range(X_SIZE)]
        return [(xr[2], 7 - s), (xr[1], 7 - s), (xr[3], 7 - s), (xr[2], s), (xr[1], s), (xr[3], s), (xr[0], 7 - s)]

    y_peers = plane_peers(z)

    def to(peer):
        return dict(device_id={"region": peer[0], "sub": peer[1]}, device_id_type=MESH)

    interior = (s > 0, s < 7)
    beside = ((g, s - 1), (g, s + 1))

    def half_load(half):
        start = pl.multiple_of(half * LANES, LANES)
        return pltpu.make_async_copy(dir_in.at[:, :, :, pl.ds(start, LANES)], dirs.at[half], dir_sem.at[half])

    loads = [
        pltpu.make_async_copy(a, b, in_sem.at[i])
        for i, (a, b) in enumerate(
            ((par_in, par), (diag_in, diag), (wt_in, wt), (left_in, left), (right_in, right), (ids_in, ids))
        )
    ]
    half_load(pe).start()
    for load in loads:
        load.start()
    barrier = pltpu.get_barrier_semaphore()

    @pl.when(is_end)
    def _():
        for peer in z_peers + y_peers:
            pl.semaphore_signal(barrier, inc=1, **to(peer))
        for source, target in DIRECT:

            @pl.when(z == target)
            def _():
                for peer in plane_peers(source):
                    pl.semaphore_signal(barrier, inc=1, **to(peer))

    for side in (0, 1):

        @pl.when(interior[side])
        def _():
            pl.semaphore_signal(barrier, inc=1, **to(beside[side]))

    half_load(1 - pe).start()
    for load in loads:
        load.wait()

    lane = iota((PIPES, LANES), 1)
    even = lax.rem(lane, 2) == 0
    lane2 = iota((PIPES, CELLS), 1)
    quarter = lax.rem(iota((PIPES, LANES), 0), 4)
    zero = jnp.zeros((PIPES, LANES), F32)

    ends = jnp.logical_or(
        jnp.logical_and(lane2 == 0, is_first), jnp.logical_and(lane2 == CELLS - 1, is_last)
    )
    for c in range(COMP):
        diag[c, c] = diag[c, c] - jnp.where(ends, 0.5, 0.0)

    def swap(v):
        return jnp.where(even, pltpu.roll(v, LANES - 1, 1), pltpu.roll(v, 1, 1))

    def nxt(v):
        return pltpu.roll(v, LANES - 1, 1)

    def lane_pack(values):
        tile = zero
        for i, v in enumerate(values):
            tile = jnp.where(lane == i, v, tile)
        return tile

    def end_cells(side):
        parts = [[zero, zero] for _ in range(NPAR)]
        for r in range(COLS):
            here = lane // 2 == r
            for k in range(NPAR):
                moved = pltpu.roll(dirs[side, k, r], (2 * r + 2 * side) % LANES, 1)
                parts[k][r % 2] = jnp.where(here, moved, parts[k][r % 2])
        tiles = [a + b for a, b in parts]
        for k in range(NPAR):
            comp[side, k] = swap(tiles[k]) if side else tiles[k]

    def end_coefficients(side, outside):
        e, n = (CELLS - 1, CELLS - 2) if side else (0, 1)
        inner, outer = (left, right) if side else (right, left)
        for t in range(COMP):
            coef[side, WT + t] = spread(wt[t, :, e : e + 1])
            for k in range(NPAR):
                coef[side, PE + NPAR * t + k] = spread(par[t, k, :, e : e + 1])
                coef[side, PN + NPAR * t + k] = spread(par[t, k, :, n : n + 1])
            for q in range(COMP):
                coef[side, DD + COMP * t + q] = spread(diag[t, q, :, e : e + 1])
                coef[side, CIN + COMP * t + q] = spread(inner[t, q, :, e : e + 1])
                if outside:
                    coef[side, COUT + COMP * t + q] = spread(outer[t, q, :, e : e + 1])

    for side, chosen in ((0, is_first), (1, is_last)):

        @pl.when(chosen)
        def _():
            row = jnp.where(g >= 16, ids[side, :, LANES:], ids[side, :, :LANES]).astype(F32)
            mine = lane == PIPES * lax.rem(g, 16) + iota((PIPES, LANES), 0)
            own = spread(jnp.sum(jnp.where(mine, row, 0.0), axis=1, keepdims=True))
            span = slice(side * LANES, side * LANES + LANES)
            inner = left if side else right
            here = [[par[t, k, :, span] for k in range(NPAR)] for t in range(COMP)]
            beyond = [[pltpu.roll(v, 1 if side else LANES - 1, 1) for v in vs] for vs in here]
            weight = [wt[t, :, span] for t in range(COMP)]
            pack = [v for vs in here for v in vs]
            for near in (True, False):
                for t in range(COMP):
                    for k in range(NPAR):
                        total = here[t][k] if near else zero
                        for q in range(COMP):
                            block, cell = (diag, here) if near else (inner, beyond)
                            total = total + block[t, q, :, span] * cell[q][k]
                        pack.append(weight[t] * total)
            pack += weight
            tile = jnp.where(lane == J_ID, own, 0.0)
            for i, v in enumerate(pack):
                tile = jnp.where(lane == i, pltpu.roll(v, (i - (LANES - 1) * side) % LANES, 1), tile)
            half_load(pe).wait()
            end_cells(side)
            for k in range(NPAR):
                jbuf[z, me, 8 * k : 8 * k + 8] = comp[side, k]
            for m in range(1, 4):
                tile = jnp.where(quarter == m, pltpu.roll(tile, J_SPAN * m, 1), tile)
            for m in range(2):
                jbuf[z, me, 16 + m : 17 + m] = jnp.sum(tile[4 * m : 4 * m + 4], axis=0, keepdims=True)
            j_own[...] = own

    def n_copy(side):
        return pltpu.make_async_remote_copy(
            src_ref=n_send.at[side],
            dst_ref=n_recv.at[1 - side],
            send_sem=ns_sem.at[side],
            recv_sem=nr_sem.at[1 - side],
            **to(beside[side]),
        )

    def n_arrival(side):
        return pltpu.make_async_remote_copy(
            src_ref=n_send.at[side],
            dst_ref=n_recv.at[side],
            send_sem=ns_sem.at[side],
            recv_sem=nr_sem.at[side],
            **to(beside[side]),
        )

    def slot(plane):
        return jbuf.at[plane, me, pl.ds(0, ROWS)]

    def z_copy(plane, peer):
        return pltpu.make_async_remote_copy(
            src_ref=slot(plane), dst_ref=slot(plane), send_sem=zs_sem, recv_sem=zr_sem.at[plane], **to(peer)
        )

    def forward(plane, peers=y_peers):
        for peer in peers:
            pltpu.make_async_remote_copy(
                src_ref=slot(plane), dst_ref=slot(plane), send_sem=ys_sem, recv_sem=yr_sem.at[plane], **to(peer)
            ).start()

    def prepare():
        half_load(1 - pe).wait()

        @pl.when(jnp.logical_not(is_end))
        def _():
            half_load(pe).wait()

        for side in (0, 1):

            @pl.when(interior[side])
            def _():
                end_cells(side)
                end_coefficients(side, True)
                source = []
                for t in range(COMP):
                    total = zero
                    for k in range(NPAR):
                        factor = jnp.where(even, coef[side, PE + NPAR * t + k], coef[side, PN + NPAR * t + k])
                        total = total + factor * comp[side, k]
                    source.append(total)
                after = [nxt(v) for v in source]
                for t in range(COMP):
                    total = source[t]
                    for q in range(COMP):
                        total = total + coef[side, DD + COMP * t + q] * source[q]
                        total = total + coef[side, CIN + COMP * t + q] * after[q]
                    src_s[side, t] = source[t]
                    n_send[side, t] = jnp.where(even, source[t], pltpu.roll(coef[side, WT + t] * total, 1, 1))
                n_send[side, COMP] = lane_pack(
                    [coef[side, COUT + i] for i in range(COMP * COMP)] + [coef[side, WT + t] for t in range(COMP)]
                )

        for side, chosen in ((0, is_first), (1, is_last)):

            @pl.when(chosen)
            def _():
                end_coefficients(side, False)

    def piece():
        def up(v):
            return jnp.where(lane2 == CELLS - 1, 0.0, pltpu.roll(v, CELLS - 1, 1))

        def down(v):
            return jnp.where(lane2 == 0, 0.0, pltpu.roll(v, 1, 1))

        p_here = [[par[t, k] for k in range(NPAR)] for t in range(COMP)]
        p_up = [[up(v) for v in vs] for vs in p_here]
        p_down = [[down(v) for v in vs] for vs in p_here]

        def product(blocks, cells, start):
            rows = []
            for t in range(COMP):
                row = []
                for k in range(NPAR):
                    total = start[t][k] if start is not None else None
                    for q in range(COMP):
                        term = blocks[t, q] * cells[q][k]
                        total = term if total is None else total + term
                    row.append(total)
                rows.append(row)
            return rows

        b0 = product(diag, p_here, p_here)
        bm = product(left, p_down, None)
        bp = product(right, p_up, None)
        weight = [wt[t] for t in range(COMP)]
        u0 = [[weight[t] * v for v in b0[t]] for t in range(COMP)]
        um = [[weight[t] * v for v in bm[t]] for t in range(COMP)]
        upl = [[weight[t] * v for v in bp[t]] for t in range(COMP)]

        def inner_sum(a, b, k, q):
            total = a[0][k] * b[0][q]
            for t in range(1, COMP):
                total = total + a[t][k] * b[t][q]
            return total

        for k in range(NPAR):
            for q in range(NPAR):
                i = NPAR * k + q
                if k <= q:
                    centre = inner_sum(b0, u0, k, q) + down(inner_sum(bp, upl, k, q)) + up(inner_sum(bm, um, k, q))
                    band[8 + i] = centre
                    if k != q:
                        band[8 + NPAR * q + k] = centre
                one = inner_sum(b0, upl, k, q) + up(inner_sum(bm, u0, k, q))
                two = up(inner_sum(bm, upl, k, q))
                band[12 + i] = one
                band[16 + i] = two
                band[4 + NPAR * q + k] = down(one)
                band[NPAR * q + k] = down(down(two))

        def wide_step(r, carry):
            shifted = []
            for k in range(NPAR):
                a = dirs[0, k, r]
                b = dirs[1, k, r]
                per_offset = []
                for off in (-2, -1, 0, 1, 2):
                    if off == 0:
                        per_offset.append((a, b))
                        continue
                    ra = pltpu.roll(a, -off % LANES, 1)
                    rb = pltpu.roll(b, -off % LANES, 1)
                    if off < 0:
                        per_offset.append((ra, jnp.where(lane < -off, ra, rb)))
                    else:
                        per_offset.append((jnp.where(lane >= LANES - off, rb, ra), rb))
                shifted.append(per_offset)
            for half in (0, 1):
                span = slice(half * LANES, half * LANES + LANES)
                for k in range(NPAR):
                    total = None
                    for o in range(5):
                        for q in range(NPAR):
                            term = band[4 * o + NPAR * k + q, :, span] * shifted[q][o][half]
                            total = term if total is None else total + term
                    hess[k, r, :, span] = total
            return carry

        lax.fori_loop(0, COLS, wide_step, 0, unroll=4)

    @pl.when(early)
    def _():
        prepare()
        piece()

    expected = jnp.where(is_end, 1 + len(z_peers) + len(y_peers), 2)
    for source, _ in DIRECT:
        expected = expected + jnp.where(jnp.logical_and(is_end, z == source), len(y_peers), 0)
    pl.semaphore_wait(barrier, expected)

    @pl.when(is_end)
    def _():
        for plane in range(Z_SIZE):

            @pl.when(z != plane)
            def _():
                z_copy(z, (x * Z_SIZE + plane, s)).start()

            for source, target in DIRECT:
                if target == plane:

                    @pl.when(z == source)
                    def _():
                        forward(z, plane_peers(target))

        forward(z)

    @pl.when(jnp.logical_not(early))
    def _():
        prepare()

    for side in (0, 1):

        @pl.when(interior[side])
        def _():
            n_copy(side).start()

    @pl.when(jnp.logical_not(early))
    def _():
        piece()

    def finish(side):
        change = [coef[side, WT + t] * mean_s[side, t] for t in range(COMP)]
        at_end, at_next = [], []
        for q in range(COMP):
            total = change[q] + mean_a[side, q]
            other = zero
            for t in range(COMP):
                total = total + coef[side, DD + COMP * t + q] * change[t]
                other = other + coef[side, CIN + COMP * t + q] * change[t]
            at_end.append(total)
            at_next.append(other)
        corr = []
        for k in range(NPAR):
            c0, c1 = zero, zero
            for t in range(COMP):
                c0 = c0 + coef[side, PE + NPAR * t + k] * at_end[t]
                c1 = c1 + coef[side, PN + NPAR * t + k] * at_next[t]
            straight = jnp.where(even, c0, pltpu.roll(c1, 1, 1))
            corr.append(swap(straight) if side else straight)
        return corr

    def add_to_piece(side, corr):
        edge = LANES - 2 if side else 0
        here = jnp.logical_and(lane >= edge, lane < edge + 2)
        span = slice(side * LANES, side * LANES + LANES)
        for r in range(COLS):
            for k in range(NPAR):
                moved = pltpu.roll(corr[k], (LANES + edge - 2 * r) % LANES, 1)
                hess[k, r, :, span] = hess[k, r, :, span] + jnp.where(here, moved, 0.0)

    @pl.when(is_end)
    def _():
        for k in reversed(Z_STEPS):
            plane = lax.rem(z + Z_SIZE - k, Z_SIZE)
            z_copy(plane, z_peers[0]).wait_recv()
            sent = z < 0
            for source, target in DIRECT:
                sent = jnp.logical_or(sent, jnp.logical_and(z == target, plane == source))

            @pl.when(jnp.logical_not(sent))
            def _():
                forward(plane)


    for side in (0, 1):

        @pl.when(interior[side])
        def _():
            n_arrival(side).wait_recv()
            theirs = n_recv[side, COMP]
            out_block = [spread(theirs[:, i : i + 1]) for i in range(COMP * COMP)]
            out_weight = [spread(theirs[:, COMP * COMP + t : COMP * COMP + t + 1]) for t in range(COMP)]
            pairs = [n_recv[side, t] for t in range(COMP)]
            adjoint = []
            for t in range(COMP):
                total, change = zero, zero
                for q in range(COMP):
                    total = total + out_block[COMP * t + q] * src_s[side, q]
                    change = change + coef[side, COUT + COMP * t + q] * pairs[q]
                adjoint.append(nxt(pairs[t]) + out_weight[t] * total)
                mean_s[side, t] = change
            for q in range(COMP):
                total = zero
                for t in range(COMP):
                    total = total + out_block[COMP * t + q] * adjoint[t]
                mean_a[side, q] = total
            add_to_piece(side, finish(side))

    @pl.when(is_end)
    def _():
        own = j_own[...]
        rows = 8 * PIPES

        def arrivals(planes, sem):
            span = jbuf.at[planes, pl.ds(0, 7), pl.ds(0, ROWS)]
            return pltpu.make_async_remote_copy(
                src_ref=span, dst_ref=span, send_sem=ys_sem, recv_sem=yr_sem.at[sem], **to(y_peers[0])
            )

        j_sum[...] = jnp.zeros_like(j_sum)
        j_weight[...] = jnp.zeros_like(j_weight)
        degree = zero
        for end in (0, 1):
            for half in (0, 1):
                row = ids[end, :, half * LANES : half * LANES + LANES].astype(F32)
                degree = degree + jnp.where(row == own, 1.0, 0.0)
        share = 1.0 / spread(jnp.sum(degree, axis=1, keepdims=True))

        def add_planes(j, carry):
            pair = [lax.rem(z + Z_SIZE - j, Z_SIZE), lax.rem(z + 1 + j, Z_SIZE)]
            columns, tiles = [], []
            for plane in pair:
                arrivals(plane, plane).wait_recv()
                halves = [jbuf[plane, :, 8 * k : 8 * k + 8].reshape(rows, LANES) for k in range(NPAR)]
                columns.append(split(jnp.concatenate(halves, axis=1)))
                for q in range(8):
                    packed = jnp.where(
                        iota((PIPES, LANES), 0) < 4, jbuf[plane, q, 16:17], jbuf[plane, q, 17:18]
                    )
                    tile = packed
                    for m in range(1, 4):
                        tile = jnp.where(quarter == m, pltpu.roll(packed, LANES - J_SPAN * m, 1), tile)
                    tiles.append(tile)
            x_parts = [jnp.concatenate([c[i] for c in columns]) for i in range(3)]
            coefs = jnp.concatenate(tiles).T
            same = coefs[J_ID : J_ID + 1] == own[:, 0:1]
            w_parts = [
                jnp.concatenate([jnp.where(same, v[i : i + 1], 0.0) for i in range(J_W)]).astype(BF16)
                for v in split(coefs[:J_SPAN], F32)
            ]
            order = ((0, 0), (0, 1), (1, 0), (0, 2), (2, 0), (1, 1))
            j_sum[...] += jnp.dot(
                jnp.concatenate([w_parts[i] for i, _ in order], axis=1),
                jnp.concatenate([x_parts[i] for _, i in order]),
                preferred_element_type=F32,
            )
            for t in range(COMP):
                j_weight[t] += jnp.where(same, coefs[J_W + t : J_W + t + 1], 0.0)
            return carry

        lax.fori_loop(0, Z_SIZE // 2, add_planes, 0)

        def part(c, k):
            return j_sum[PIPES * c : PIPES * c + PIPES, LANES * k : LANES * k + LANES]

        for t in range(COMP):
            c = NPAR * t
            mean = share * (part(c, 0) + part(c + 1, 1))
            near = part(8 + c, 0) + part(9 + c, 1)
            far = part(16 + c, 0) + part(17 + c, 1)
            weights = spread(jnp.sum(j_weight[t], axis=1, keepdims=True))
            mean_s[pe, t] = 0.5 * mean
            mean_a[pe, t] = 0.5 * share * (near + nxt(far) + 0.5 * weights * mean)
        for side, chosen in ((0, is_first), (1, is_last)):

            @pl.when(chosen)
            def _():
                for k, v in enumerate(finish(side)):
                    last[k] = v

        for plane in range(Z_SIZE):
            sent = z < 0
            for source, target in DIRECT:
                if source == plane:
                    sent = jnp.logical_or(sent, z == target)

            @pl.when(jnp.logical_not(sent))
            def _():
                arrivals(plane, plane).wait_send()

        for source, target in DIRECT:

            @pl.when(z == source)
            def _():
                arrivals(target, target).wait_send()

        span = jbuf.at[0, pl.ds(0, 7), pl.ds(0, ROWS)]
        pltpu.make_async_remote_copy(
            src_ref=span, dst_ref=span, send_sem=zs_sem, recv_sem=yr_sem.at[0], **to(z_peers[0])
        ).wait_send()

    for side in (0, 1):

        @pl.when(interior[side])
        def _():
            n_copy(side).wait_send()


def write_kernel(hess, last, out, piece, sem):
    s = lax.axis_index("sub")
    lane = iota((PIPES, LANES), 1)

    def write(side, k, source):
        span = pl.ds(side * LANES, LANES)
        return pltpu.make_async_copy(source, out.at[k, :, :, span], sem.at[side, k])

    for side in (0, 1):

        @pl.when(s != 7 * side)
        def _():
            for k in range(NPAR):
                write(side, k, hess.at[k, :, :, pl.ds(side * LANES, LANES)]).start()

    for side in (0, 1):

        @pl.when(s == 7 * side)
        def _():
            edge = LANES - 2 if side else 0
            here = jnp.logical_and(lane >= edge, lane < edge + 2)
            for k in range(NPAR):
                corr = last[k]
                for r in range(COLS):
                    moved = pltpu.roll(corr, (LANES + edge - 2 * r) % LANES, 1)
                    piece[k, r] = hess[k, r, :, side * LANES : side * LANES + LANES] + jnp.where(here, moved, 0.0)
                write(side, k, piece.at[k]).start()

    for side in (0, 1):
        for k in range(NPAR):
            write(side, k, piece.at[k]).wait()


def on_device(directions, diag_blocks, left_blocks, right_blocks, param_blocks, obs_weight, end_junction):
    args = (directions, diag_blocks, left_blocks, right_blocks, param_blocks, obs_weight, jnp.swapaxes(end_junction, 1, 2))
    args = tuple(pltpu.with_memory_space_constraint(a, pltpu.HBM) for a in args)
    dma = pltpu.SemaphoreType.DMA

    def tiles(*counts):
        return pltpu.VMEM(counts + (PIPES, LANES), F32)

    hess, last = pl.pallas_call(
        kernel,
        out_shape=(pltpu.VMEM(directions.shape, F32), tiles(NPAR)),
        in_specs=[pl.BlockSpec(memory_space=pl.ANY)] * len(args),
        out_specs=[pl.BlockSpec(memory_space=pltpu.VMEM)] * 2,
        scratch_shapes=[tiles(2, NPAR, COLS)]
        + [pltpu.VMEM(a.shape, a.dtype) for a in args[1:]]
        + [
            pltpu.VMEM((5 * NPAR * NPAR, PIPES, CELLS), F32),
            tiles(2, N_COEF),
            tiles(2, NPAR),
            tiles(2, COMP),
            tiles(2, COMP + 1),
            tiles(2, COMP + 1),
            pltpu.VMEM((Z_SIZE, 8, 24, LANES), F32),
            pltpu.VMEM((PIPES * J_W, 2 * LANES), F32),
            tiles(COMP),
            tiles(),
            tiles(2, COMP),
            tiles(2, COMP),
            dma((2,)),
            dma((6,)),
            dma((2,)),
            dma((2,)),
            dma,
            dma((8,)),
            dma,
            dma((8,)),
        ],
        compiler_params=pltpu.CompilerParams(
            collective_id=3, has_side_effects=True, vmem_limit_bytes=56 * 1024 * 1024
        ),
    )(*args)
    return pl.pallas_call(
        write_kernel,
        out_shape=jax.ShapeDtypeStruct(directions.shape, F32),
        in_specs=[pl.BlockSpec(memory_space=pltpu.VMEM)] * 2,
        out_specs=pl.BlockSpec(memory_space=pl.ANY),
        scratch_shapes=[tiles(NPAR, COLS), dma((2, NPAR))],
    )(*(pltpu.with_memory_space_constraint(v, pltpu.VMEM) for v in (hess, last)))


def solution(mesh):
    return jax.shard_map(
        on_device,
        mesh=mesh,
        in_specs=(
            P(None, None, "region", "sub"),
            P(None, None, "region", "sub"),
            P(None, None, "region", "sub"),
            P(None, None, "region", "sub"),
            P(None, None, "region", "sub"),
            P(None, "region", "sub"),
            P(),
        ),
        out_specs=P(None, None, "region", "sub"),
        check_vma=False,
    )
```

```python
import jax
import jax.numpy as jnp
from jax import lax
from jax.experimental import pallas as pl
from jax.experimental.pallas import tpu as pltpu
from jax.sharding import PartitionSpec as P

MESH = pl.DeviceIdType.MESH
F32 = jnp.float32
BF16 = jnp.bfloat16
X_SIZE, Z_SIZE = 4, 8
COMP, NPAR, COLS, PIPES, CELLS = 4, 2, 64, 8, 256
LANES = 128
Z_STEPS = (4, 3, 5, 2, 6, 1, 7)
DIRECT = ((4, 0), (3, 0), (5, 1))
PE, PN, DD, CIN, COUT, WT = 0, 8, 16, 32, 48, 64
N_COEF = 68
J_W, J_ID, J_SPAN = 24, 28, 32
ROWS = 18


def iota(shape, dim):
    return lax.broadcasted_iota(jnp.int32, shape, dim)


def split(v, kind=BF16):
    parts = []
    for _ in range(3):
        part = v.astype(BF16)
        v = v - part.astype(F32)
        parts.append(part.astype(kind))
    return parts


def spread(column):
    return jnp.broadcast_to(column, (PIPES, LANES))


def kernel(
    dir_in, diag_in, left_in, right_in, par_in, wt_in, ids_in, hess, last,
    dirs, diag, left, right, par, wt, ids,
    band, coef, comp, src_s, n_send, n_recv, jbuf, j_sum, j_weight, j_own, mean_s, mean_a,
    dir_sem, in_sem, ns_sem, nr_sem, zs_sem, zr_sem, ys_sem, yr_sem,
):
    g = lax.axis_index("region")
    s = lax.axis_index("sub")
    x, z = g // Z_SIZE, lax.rem(g, Z_SIZE)
    me = 2 * x + s // 7
    is_first, is_last = s == 0, s == 7
    is_end = jnp.logical_or(is_first, is_last)
    early = jnp.logical_and(is_end, z < Z_SIZE // 2)
    pe = s // 7

    z_peers = [(x * Z_SIZE + lax.rem(z + k, Z_SIZE), s) for k in Z_STEPS]

    def plane_peers(plane):
        xr = [lax.rem(x + k, X_SIZE) * Z_SIZE + plane for k in range(X_SIZE)]
        return [(xr[2], 7 - s), (xr[1], 7 - s), (xr[3], 7 - s), (xr[2], s), (xr[1], s), (xr[3], s), (xr[0], 7 - s)]

    y_peers = plane_peers(z)

    def to(peer):
        return dict(device_id={"region": peer[0], "sub": peer[1]}, device_id_type=MESH)

    interior = (s > 0, s < 7)
    beside = ((g, s - 1), (g, s + 1))

    def half_load(half):
        start = pl.multiple_of(half * LANES, LANES)
        return pltpu.make_async_copy(dir_in.at[:, :, :, pl.ds(start, LANES)], dirs.at[half], dir_sem.at[half])

    loads = [
        pltpu.make_async_copy(a, b, in_sem.at[i])
        for i, (a, b) in enumerate(
            ((par_in, par), (diag_in, diag), (wt_in, wt), (left_in, left), (right_in, right), (ids_in, ids))
        )
    ]
    half_load(pe).start()
    for load in loads:
        load.start()
    barrier = pltpu.get_barrier_semaphore()

    @pl.when(is_end)
    def _():
        for peer in z_peers + y_peers:
            pl.semaphore_signal(barrier, inc=1, **to(peer))
        for source, target in DIRECT:

            @pl.when(z == target)
            def _():
                for peer in plane_peers(source):
                    pl.semaphore_signal(barrier, inc=1, **to(peer))

    for side in (0, 1):

        @pl.when(interior[side])
        def _():
            pl.semaphore_signal(barrier, inc=1, **to(beside[side]))

    half_load(1 - pe).start()
    for load in loads:
        load.wait()

    lane = iota((PIPES, LANES), 1)
    even = lax.rem(lane, 2) == 0
    lane2 = iota((PIPES, CELLS), 1)
    quarter = lax.rem(iota((PIPES, LANES), 0), 4)
    zero = jnp.zeros((PIPES, LANES), F32)

    ends = jnp.logical_or(
        jnp.logical_and(lane2 == 0, is_first), jnp.logical_and(lane2 == CELLS - 1, is_last)
    )
    for c in range(COMP):
        diag[c, c] = diag[c, c] - jnp.where(ends, 0.5, 0.0)

    def swap(v):
        return jnp.where(even, pltpu.roll(v, LANES - 1, 1), pltpu.roll(v, 1, 1))

    def nxt(v):
        return pltpu.roll(v, LANES - 1, 1)

    def lane_pack(values):
        tile = zero
        for i, v in enumerate(values):
            tile = jnp.where(lane == i, v, tile)
        return tile

    def end_cells(side):
        parts = [[zero, zero] for _ in range(NPAR)]
        for r in range(COLS):
            here = lane // 2 == r
            for k in range(NPAR):
                moved = pltpu.roll(dirs[side, k, r], (2 * r + 2 * side) % LANES, 1)
                parts[k][r % 2] = jnp.where(here, moved, parts[k][r % 2])
        tiles = [a + b for a, b in parts]
        for k in range(NPAR):
            comp[side, k] = swap(tiles[k]) if side else tiles[k]

    def end_coefficients(side, outside):
        e, n = (CELLS - 1, CELLS - 2) if side else (0, 1)
        inner, outer = (left, right) if side else (right, left)
        for t in range(COMP):
            coef[side, WT + t] = spread(wt[t, :, e : e + 1])
            for k in range(NPAR):
                coef[side, PE + NPAR * t + k] = spread(par[t, k, :, e : e + 1])
                coef[side, PN + NPAR * t + k] = spread(par[t, k, :, n : n + 1])
            for q in range(COMP):
                coef[side, DD + COMP * t + q] = spread(diag[t, q, :, e : e + 1])
                coef[side, CIN + COMP * t + q] = spread(inner[t, q, :, e : e + 1])
                if outside:
                    coef[side, COUT + COMP * t + q] = spread(outer[t, q, :, e : e + 1])

    for side, chosen in ((0, is_first), (1, is_last)):

        @pl.when(chosen)
        def _():
            row = jnp.where(g >= 16, ids[side, :, LANES:], ids[side, :, :LANES]).astype(F32)
            mine = lane == PIPES * lax.rem(g, 16) + iota((PIPES, LANES), 0)
            own = spread(jnp.sum(jnp.where(mine, row, 0.0), axis=1, keepdims=True))
            span = slice(side * LANES, side * LANES + LANES)
            inner = left if side else right
            here = [[par[t, k, :, span] for k in range(NPAR)] for t in range(COMP)]
            beyond = [[pltpu.roll(v, 1 if side else LANES - 1, 1) for v in vs] for vs in here]
            weight = [wt[t, :, span] for t in range(COMP)]
            pack = [v for vs in here for v in vs]
            for near in (True, False):
                for t in range(COMP):
                    for k in range(NPAR):
                        total = here[t][k] if near else zero
                        for q in range(COMP):
                            block, cell = (diag, here) if near else (inner, beyond)
                            total = total + block[t, q, :, span] * cell[q][k]
                        pack.append(weight[t] * total)
            pack += weight
            tile = jnp.where(lane == J_ID, own, 0.0)
            for i, v in enumerate(pack):
                tile = jnp.where(lane == i, pltpu.roll(v, (i - (LANES - 1) * side) % LANES, 1), tile)
            half_load(pe).wait()
            end_cells(side)
            for k in range(NPAR):
                jbuf[z, me, 8 * k : 8 * k + 8] = comp[side, k]
            for m in range(1, 4):
                tile = jnp.where(quarter == m, pltpu.roll(tile, J_SPAN * m, 1), tile)
            for m in range(2):
                jbuf[z, me, 16 + m : 17 + m] = jnp.sum(tile[4 * m : 4 * m + 4], axis=0, keepdims=True)
            j_own[...] = own

    def n_copy(side):
        return pltpu.make_async_remote_copy(
            src_ref=n_send.at[side],
            dst_ref=n_recv.at[1 - side],
            send_sem=ns_sem.at[side],
            recv_sem=nr_sem.at[1 - side],
            **to(beside[side]),
        )

    def n_arrival(side):
        return pltpu.make_async_remote_copy(
            src_ref=n_send.at[side],
            dst_ref=n_recv.at[side],
            send_sem=ns_sem.at[side],
            recv_sem=nr_sem.at[side],
            **to(beside[side]),
        )

    def slot(plane):
        return jbuf.at[plane, me, pl.ds(0, ROWS)]

    def z_copy(plane, peer):
        return pltpu.make_async_remote_copy(
            src_ref=slot(plane), dst_ref=slot(plane), send_sem=zs_sem, recv_sem=zr_sem.at[plane], **to(peer)
        )

    def went_straight(plane):
        answer = z < 0
        for source, target in DIRECT:
            answer = jnp.logical_or(answer, jnp.logical_and(z == target, plane == source))
        return answer

    def forward(plane, peers=y_peers):
        for peer in peers:
            pltpu.make_async_remote_copy(
                src_ref=slot(plane), dst_ref=slot(plane), send_sem=ys_sem, recv_sem=yr_sem.at[plane], **to(peer)
            ).start()

    def prepare():
        half_load(1 - pe).wait()

        @pl.when(jnp.logical_not(is_end))
        def _():
            half_load(pe).wait()

        for side in (0, 1):

            @pl.when(interior[side])
            def _():
                end_cells(side)
                end_coefficients(side, True)
                source = []
                for t in range(COMP):
                    total = zero
                    for k in range(NPAR):
                        factor = jnp.where(even, coef[side, PE + NPAR * t + k], coef[side, PN + NPAR * t + k])
                        total = total + factor * comp[side, k]
                    source.append(total)
                after = [nxt(v) for v in source]
                for t in range(COMP):
                    total = source[t]
                    for q in range(COMP):
                        total = total + coef[side, DD + COMP * t + q] * source[q]
                        total = total + coef[side, CIN + COMP * t + q] * after[q]
                    src_s[side, t] = source[t]
                    n_send[side, t] = jnp.where(even, source[t], pltpu.roll(coef[side, WT + t] * total, 1, 1))
                n_send[side, COMP] = lane_pack(
                    [coef[side, COUT + i] for i in range(COMP * COMP)] + [coef[side, WT + t] for t in range(COMP)]
                )

        for side, chosen in ((0, is_first), (1, is_last)):

            @pl.when(chosen)
            def _():
                end_coefficients(side, False)

    def piece():
        def up(v):
            return jnp.where(lane2 == CELLS - 1, 0.0, pltpu.roll(v, CELLS - 1, 1))

        def down(v):
            return jnp.where(lane2 == 0, 0.0, pltpu.roll(v, 1, 1))

        p_here = [[par[t, k] for k in range(NPAR)] for t in range(COMP)]
        p_up = [[up(v) for v in vs] for vs in p_here]
        p_down = [[down(v) for v in vs] for vs in p_here]

        def product(blocks, cells, start):
            rows = []
            for t in range(COMP):
                row = []
                for k in range(NPAR):
                    total = start[t][k] if start is not None else None
                    for q in range(COMP):
                        term = blocks[t, q] * cells[q][k]
                        total = term if total is None else total + term
                    row.append(total)
                rows.append(row)
            return rows

        b0 = product(diag, p_here, p_here)
        bm = product(left, p_down, None)
        bp = product(right, p_up, None)
        weight = [wt[t] for t in range(COMP)]
        u0 = [[weight[t] * v for v in b0[t]] for t in range(COMP)]
        um = [[weight[t] * v for v in bm[t]] for t in range(COMP)]
        upl = [[weight[t] * v for v in bp[t]] for t in range(COMP)]

        def inner_sum(a, b, k, q):
            total = a[0][k] * b[0][q]
            for t in range(1, COMP):
                total = total + a[t][k] * b[t][q]
            return total

        for k in range(NPAR):
            for q in range(NPAR):
                i = NPAR * k + q
                if k <= q:
                    centre = inner_sum(b0, u0, k, q) + down(inner_sum(bp, upl, k, q)) + up(inner_sum(bm, um, k, q))
                    band[8 + i] = centre
                    if k != q:
                        band[8 + NPAR * q + k] = centre
                one = inner_sum(b0, upl, k, q) + up(inner_sum(bm, u0, k, q))
                two = up(inner_sum(bm, upl, k, q))
                band[12 + i] = one
                band[16 + i] = two
                band[4 + NPAR * q + k] = down(one)
                band[NPAR * q + k] = down(down(two))

        def wide_step(r, carry):
            shifted = []
            for k in range(NPAR):
                a = dirs[0, k, r]
                b = dirs[1, k, r]
                per_offset = []
                for off in (-2, -1, 0, 1, 2):
                    if off == 0:
                        per_offset.append((a, b))
                        continue
                    ra = pltpu.roll(a, -off % LANES, 1)
                    rb = pltpu.roll(b, -off % LANES, 1)
                    if off < 0:
                        per_offset.append((ra, jnp.where(lane < -off, ra, rb)))
                    else:
                        per_offset.append((jnp.where(lane >= LANES - off, rb, ra), rb))
                shifted.append(per_offset)
            for half in (0, 1):
                span = slice(half * LANES, half * LANES + LANES)
                for k in range(NPAR):
                    total = None
                    for o in range(5):
                        for q in range(NPAR):
                            term = band[4 * o + NPAR * k + q, :, span] * shifted[q][o][half]
                            total = term if total is None else total + term
                    hess[k, r, :, span] = total
            return carry

        lax.fori_loop(0, COLS, wide_step, 0, unroll=4)

    @pl.when(early)
    def _():
        prepare()
        piece()

    expected = jnp.where(is_end, 1 + len(z_peers) + len(y_peers), 2)
    for source, _ in DIRECT:
        expected = expected + jnp.where(jnp.logical_and(is_end, z == source), len(y_peers), 0)
    pl.semaphore_wait(barrier, expected)

    @pl.when(is_end)
    def _():
        for plane in range(Z_SIZE):

            @pl.when(z != plane)
            def _():
                z_copy(z, (x * Z_SIZE + plane, s)).start()

        for source, target in DIRECT:

            @pl.when(z == source)
            def _():
                forward(z, plane_peers(target))

        forward(z)

    @pl.when(jnp.logical_not(early))
    def _():
        prepare()

    for side in (0, 1):

        @pl.when(interior[side])
        def _():
            n_copy(side).start()

    @pl.when(jnp.logical_not(early))
    def _():
        piece()

    def finish(side):
        change = [coef[side, WT + t] * mean_s[side, t] for t in range(COMP)]
        at_end, at_next = [], []
        for q in range(COMP):
            total = change[q] + mean_a[side, q]
            other = zero
            for t in range(COMP):
                total = total + coef[side, DD + COMP * t + q] * change[t]
                other = other + coef[side, CIN + COMP * t + q] * change[t]
            at_end.append(total)
            at_next.append(other)
        corr = []
        for k in range(NPAR):
            c0, c1 = zero, zero
            for t in range(COMP):
                c0 = c0 + coef[side, PE + NPAR * t + k] * at_end[t]
                c1 = c1 + coef[side, PN + NPAR * t + k] * at_next[t]
            straight = jnp.where(even, c0, pltpu.roll(c1, 1, 1))
            corr.append(swap(straight) if side else straight)
        return corr

    def add_to_piece(side, corr):
        edge = LANES - 2 if side else 0
        here = jnp.logical_and(lane >= edge, lane < edge + 2)
        span = slice(side * LANES, side * LANES + LANES)
        for r in range(COLS):
            for k in range(NPAR):
                moved = pltpu.roll(corr[k], (LANES + edge - 2 * r) % LANES, 1)
                hess[k, r, :, span] = hess[k, r, :, span] + jnp.where(here, moved, 0.0)

    def beside_part():
        for side in (0, 1):

            @pl.when(interior[side])
            def _():
                n_arrival(side).wait_recv()
                theirs = n_recv[side, COMP]
                out_block = [spread(theirs[:, i : i + 1]) for i in range(COMP * COMP)]
                out_weight = [spread(theirs[:, COMP * COMP + t : COMP * COMP + t + 1]) for t in range(COMP)]
                pairs = [n_recv[side, t] for t in range(COMP)]
                adjoint = []
                for t in range(COMP):
                    total, change = zero, zero
                    for q in range(COMP):
                        total = total + out_block[COMP * t + q] * src_s[side, q]
                        change = change + coef[side, COUT + COMP * t + q] * pairs[q]
                    adjoint.append(nxt(pairs[t]) + out_weight[t] * total)
                    mean_s[side, t] = change
                for q in range(COMP):
                    total = zero
                    for t in range(COMP):
                        total = total + out_block[COMP * t + q] * adjoint[t]
                    mean_a[side, q] = total
                add_to_piece(side, finish(side))

    pl.when(early)(beside_part)

    @pl.when(is_end)
    def _():
        for k in reversed(Z_STEPS):
            plane = lax.rem(z + Z_SIZE - k, Z_SIZE)

            @pl.when(jnp.logical_not(went_straight(plane)))
            def _():
                z_copy(plane, z_peers[0]).wait_recv()
                forward(plane)


    pl.when(jnp.logical_not(early))(beside_part)

    @pl.when(is_end)
    def _():
        own = j_own[...]
        rows = 8 * PIPES

        def arrivals(planes, sem):
            span = jbuf.at[planes, pl.ds(0, 7), pl.ds(0, ROWS)]
            return pltpu.make_async_remote_copy(
                src_ref=span, dst_ref=span, send_sem=ys_sem, recv_sem=yr_sem.at[sem], **to(y_peers[0])
            )

        j_sum[...] = jnp.zeros_like(j_sum)
        j_weight[...] = jnp.zeros_like(j_weight)
        degree = zero
        for end in (0, 1):
            for half in (0, 1):
                row = ids[end, :, half * LANES : half * LANES + LANES].astype(F32)
                degree = degree + jnp.where(row == own, 1.0, 0.0)
        share = 1.0 / spread(jnp.sum(degree, axis=1, keepdims=True))

        def add_planes(j, carry):
            pair = [lax.rem(z + Z_SIZE - j, Z_SIZE), lax.rem(z + 1 + j, Z_SIZE)]
            columns, tiles = [], []
            for plane in pair:
                arrivals(plane, plane).wait_recv()

                @pl.when(went_straight(plane))
                def _():
                    z_copy(plane, z_peers[0]).wait_recv()

                halves = [jbuf[plane, :, 8 * k : 8 * k + 8].reshape(rows, LANES) for k in range(NPAR)]
                columns.append(split(jnp.concatenate(halves, axis=1)))
                for q in range(8):
                    packed = jnp.where(
                        iota((PIPES, LANES), 0) < 4, jbuf[plane, q, 16:17], jbuf[plane, q, 17:18]
                    )
                    tile = packed
                    for m in range(1, 4):
                        tile = jnp.where(quarter == m, pltpu.roll(packed, LANES - J_SPAN * m, 1), tile)
                    tiles.append(tile)
            x_parts = [jnp.concatenate([c[i] for c in columns]) for i in range(3)]
            coefs = jnp.concatenate(tiles).T
            same = coefs[J_ID : J_ID + 1] == own[:, 0:1]
            w_parts = [
                jnp.concatenate([jnp.where(same, v[i : i + 1], 0.0) for i in range(J_W)]).astype(BF16)
                for v in split(coefs[:J_SPAN], F32)
            ]
            order = ((0, 0), (0, 1), (1, 0), (0, 2), (2, 0), (1, 1))
            j_sum[...] += jnp.dot(
                jnp.concatenate([w_parts[i] for i, _ in order], axis=1),
                jnp.concatenate([x_parts[i] for _, i in order]),
                preferred_element_type=F32,
            )
            for t in range(COMP):
                j_weight[t] += jnp.where(same, coefs[J_W + t : J_W + t + 1], 0.0)
            return carry

        lax.fori_loop(0, Z_SIZE // 2, add_planes, 0)

        def part(c, k):
            return j_sum[PIPES * c : PIPES * c + PIPES, LANES * k : LANES * k + LANES]

        for t in range(COMP):
            c = NPAR * t
            mean = share * (part(c, 0) + part(c + 1, 1))
            near = part(8 + c, 0) + part(9 + c, 1)
            far = part(16 + c, 0) + part(17 + c, 1)
            weights = spread(jnp.sum(j_weight[t], axis=1, keepdims=True))
            mean_s[pe, t] = 0.5 * mean
            mean_a[pe, t] = 0.5 * share * (near + nxt(far) + 0.5 * weights * mean)
        for side, chosen in ((0, is_first), (1, is_last)):

            @pl.when(chosen)
            def _():
                for k, v in enumerate(finish(side)):
                    last[k] = v

        for plane in range(Z_SIZE):
            sent = z < 0
            for source, target in DIRECT:
                if source == plane:
                    sent = jnp.logical_or(sent, z == target)

            @pl.when(jnp.logical_not(sent))
            def _():
                arrivals(plane, plane).wait_send()

        for source, target in DIRECT:

            @pl.when(z == source)
            def _():
                arrivals(target, target).wait_send()

        span = jbuf.at[0, pl.ds(0, 7), pl.ds(0, ROWS)]
        pltpu.make_async_remote_copy(
            src_ref=span, dst_ref=span, send_sem=zs_sem, recv_sem=yr_sem.at[0], **to(z_peers[0])
        ).wait_send()

    for side in (0, 1):

        @pl.when(interior[side])
        def _():
            n_copy(side).wait_send()


def write_kernel(hess, last, out, piece, sem):
    s = lax.axis_index("sub")
    lane = iota((PIPES, LANES), 1)

    def write(side, k, source):
        span = pl.ds(side * LANES, LANES)
        return pltpu.make_async_copy(source, out.at[k, :, :, span], sem.at[side, k])

    for side in (0, 1):

        @pl.when(s != 7 * side)
        def _():
            for k in range(NPAR):
                write(side, k, hess.at[k, :, :, pl.ds(side * LANES, LANES)]).start()

    for side in (0, 1):

        @pl.when(s == 7 * side)
        def _():
            edge = LANES - 2 if side else 0
            here = jnp.logical_and(lane >= edge, lane < edge + 2)
            for k in range(NPAR):
                corr = last[k]
                for r in range(COLS):
                    moved = pltpu.roll(corr, (LANES + edge - 2 * r) % LANES, 1)
                    piece[k, r] = hess[k, r, :, side * LANES : side * LANES + LANES] + jnp.where(here, moved, 0.0)
                write(side, k, piece.at[k]).start()

    for side in (0, 1):
        for k in range(NPAR):
            write(side, k, piece.at[k]).wait()


def on_device(directions, diag_blocks, left_blocks, right_blocks, param_blocks, obs_weight, end_junction):
    args = (directions, diag_blocks, left_blocks, right_blocks, param_blocks, obs_weight, jnp.swapaxes(end_junction, 1, 2))
    args = tuple(pltpu.with_memory_space_constraint(a, pltpu.HBM) for a in args)
    dma = pltpu.SemaphoreType.DMA

    def tiles(*counts):
        return pltpu.VMEM(counts + (PIPES, LANES), F32)

    hess, last = pl.pallas_call(
        kernel,
        out_shape=(pltpu.VMEM(directions.shape, F32), tiles(NPAR)),
        in_specs=[pl.BlockSpec(memory_space=pl.ANY)] * len(args),
        out_specs=[pl.BlockSpec(memory_space=pltpu.VMEM)] * 2,
        scratch_shapes=[tiles(2, NPAR, COLS)]
        + [pltpu.VMEM(a.shape, a.dtype) for a in args[1:]]
        + [
            pltpu.VMEM((5 * NPAR * NPAR, PIPES, CELLS), F32),
            tiles(2, N_COEF),
            tiles(2, NPAR),
            tiles(2, COMP),
            tiles(2, COMP + 1),
            tiles(2, COMP + 1),
            pltpu.VMEM((Z_SIZE, 8, 24, LANES), F32),
            pltpu.VMEM((PIPES * J_W, 2 * LANES), F32),
            tiles(COMP),
            tiles(),
            tiles(2, COMP),
            tiles(2, COMP),
            dma((2,)),
            dma((6,)),
            dma((2,)),
            dma((2,)),
            dma,
            dma((8,)),
            dma,
            dma((8,)),
        ],
        compiler_params=pltpu.CompilerParams(
            collective_id=3, has_side_effects=True, vmem_limit_bytes=56 * 1024 * 1024
        ),
    )(*args)
    return pl.pallas_call(
        write_kernel,
        out_shape=jax.ShapeDtypeStruct(directions.shape, F32),
        in_specs=[pl.BlockSpec(memory_space=pltpu.VMEM)] * 2,
        out_specs=pl.BlockSpec(memory_space=pl.ANY),
        scratch_shapes=[tiles(NPAR, COLS), dma((2, NPAR))],
    )(*(pltpu.with_memory_space_constraint(v, pltpu.VMEM) for v in (hess, last)))


def solution(mesh):
    return jax.shard_map(
        on_device,
        mesh=mesh,
        in_specs=(
            P(None, None, "region", "sub"),
            P(None, None, "region", "sub"),
            P(None, None, "region", "sub"),
            P(None, None, "region", "sub"),
            P(None, None, "region", "sub"),
            P(None, "region", "sub"),
            P(),
        ),
        out_specs=P(None, None, "region", "sub"),
        check_vma=False,
    )
```

```python
import jax
import jax.numpy as jnp
from jax import lax
from jax.experimental import pallas as pl
from jax.experimental.pallas import tpu as pltpu
from jax.sharding import PartitionSpec as P

MESH = pl.DeviceIdType.MESH
F32 = jnp.float32
BF16 = jnp.bfloat16
X_SIZE, Z_SIZE = 4, 8
COMP, NPAR, COLS, PIPES, CELLS = 4, 2, 64, 8, 256
LANES = 128
Z_STEPS = (4, 3, 5, 2, 6, 1, 7)
DIRECT = ((4, 0), (3, 0), (5, 1), (6, 2))
PE, PN, DD, CIN, COUT, WT = 0, 8, 16, 32, 48, 64
N_COEF = 68
J_W, J_ID, J_SPAN = 24, 28, 32
ROWS = 18


def iota(shape, dim):
    return lax.broadcasted_iota(jnp.int32, shape, dim)


def split(v, kind=BF16):
    parts = []
    for _ in range(3):
        part = v.astype(BF16)
        v = v - part.astype(F32)
        parts.append(part.astype(kind))
    return parts


def spread(column):
    return jnp.broadcast_to(column, (PIPES, LANES))


def kernel(
    dir_in, diag_in, left_in, right_in, par_in, wt_in, ids_in, hess, last,
    dirs, diag, left, right, par, wt, ids,
    band, coef, comp, src_s, n_send, n_recv, jbuf, j_sum, j_weight, j_own, mean_s, mean_a,
    dir_sem, in_sem, ns_sem, nr_sem, zs_sem, zr_sem, ys_sem, yr_sem,
):
    g = lax.axis_index("region")
    s = lax.axis_index("sub")
    x, z = g // Z_SIZE, lax.rem(g, Z_SIZE)
    me = 2 * x + s // 7
    is_first, is_last = s == 0, s == 7
    is_end = jnp.logical_or(is_first, is_last)
    early = jnp.logical_and(is_end, z < Z_SIZE // 2)
    pe = s // 7

    z_peers = [(x * Z_SIZE + lax.rem(z + k, Z_SIZE), s) for k in Z_STEPS]

    def plane_peers(plane):
        xr = [lax.rem(x + k, X_SIZE) * Z_SIZE + plane for k in range(X_SIZE)]
        return [(xr[2], 7 - s), (xr[1], 7 - s), (xr[3], 7 - s), (xr[2], s), (xr[1], s), (xr[3], s), (xr[0], 7 - s)]

    y_peers = plane_peers(z)

    def to(peer):
        return dict(device_id={"region": peer[0], "sub": peer[1]}, device_id_type=MESH)

    interior = (s > 0, s < 7)
    beside = ((g, s - 1), (g, s + 1))

    def half_load(half):
        start = pl.multiple_of(half * LANES, LANES)
        return pltpu.make_async_copy(dir_in.at[:, :, :, pl.ds(start, LANES)], dirs.at[half], dir_sem.at[half])

    loads = [
        pltpu.make_async_copy(a, b, in_sem.at[i])
        for i, (a, b) in enumerate(
            ((par_in, par), (diag_in, diag), (wt_in, wt), (left_in, left), (right_in, right), (ids_in, ids))
        )
    ]
    half_load(pe).start()
    for load in loads:
        load.start()
    barrier = pltpu.get_barrier_semaphore()

    @pl.when(is_end)
    def _():
        for peer in z_peers + y_peers:
            pl.semaphore_signal(barrier, inc=1, **to(peer))
        for source, target in DIRECT:

            @pl.when(z == target)
            def _():
                for peer in plane_peers(source):
                    pl.semaphore_signal(barrier, inc=1, **to(peer))

    for side in (0, 1):

        @pl.when(interior[side])
        def _():
            pl.semaphore_signal(barrier, inc=1, **to(beside[side]))

    half_load(1 - pe).start()
    for load in loads:
        load.wait()

    lane = iota((PIPES, LANES), 1)
    even = lax.rem(lane, 2) == 0
    lane2 = iota((PIPES, CELLS), 1)
    quarter = lax.rem(iota((PIPES, LANES), 0), 4)
    zero = jnp.zeros((PIPES, LANES), F32)

    ends = jnp.logical_or(
        jnp.logical_and(lane2 == 0, is_first), jnp.logical_and(lane2 == CELLS - 1, is_last)
    )
    for c in range(COMP):
        diag[c, c] = diag[c, c] - jnp.where(ends, 0.5, 0.0)

    def swap(v):
        return jnp.where(even, pltpu.roll(v, LANES - 1, 1), pltpu.roll(v, 1, 1))

    def nxt(v):
        return pltpu.roll(v, LANES - 1, 1)

    def lane_pack(values):
        tile = zero
        for i, v in enumerate(values):
            tile = jnp.where(lane == i, v, tile)
        return tile

    def end_cells(side):
        parts = [[zero, zero] for _ in range(NPAR)]
        for r in range(COLS):
            here = lane // 2 == r
            for k in range(NPAR):
                moved = pltpu.roll(dirs[side, k, r], (2 * r + 2 * side) % LANES, 1)
                parts[k][r % 2] = jnp.where(here, moved, parts[k][r % 2])
        tiles = [a + b for a, b in parts]
        for k in range(NPAR):
            comp[side, k] = swap(tiles[k]) if side else tiles[k]

    def end_coefficients(side, outside):
        e, n = (CELLS - 1, CELLS - 2) if side else (0, 1)
        inner, outer = (left, right) if side else (right, left)
        for t in range(COMP):
            coef[side, WT + t] = spread(wt[t, :, e : e + 1])
            for k in range(NPAR):
                coef[side, PE + NPAR * t + k] = spread(par[t, k, :, e : e + 1])
                coef[side, PN + NPAR * t + k] = spread(par[t, k, :, n : n + 1])
            for q in range(COMP):
                coef[side, DD + COMP * t + q] = spread(diag[t, q, :, e : e + 1])
                coef[side, CIN + COMP * t + q] = spread(inner[t, q, :, e : e + 1])
                if outside:
                    coef[side, COUT + COMP * t + q] = spread(outer[t, q, :, e : e + 1])

    for side, chosen in ((0, is_first), (1, is_last)):

        @pl.when(chosen)
        def _():
            row = jnp.where(g >= 16, ids[side, :, LANES:], ids[side, :, :LANES]).astype(F32)
            mine = lane == PIPES * lax.rem(g, 16) + iota((PIPES, LANES), 0)
            own = spread(jnp.sum(jnp.where(mine, row, 0.0), axis=1, keepdims=True))
            span = slice(side * LANES, side * LANES + LANES)
            inner = left if side else right
            here = [[par[t, k, :, span] for k in range(NPAR)] for t in range(COMP)]
            beyond = [[pltpu.roll(v, 1 if side else LANES - 1, 1) for v in vs] for vs in here]
            weight = [wt[t, :, span] for t in range(COMP)]
            pack = [v for vs in here for v in vs]
            for near in (True, False):
                for t in range(COMP):
                    for k in range(NPAR):
                        total = here[t][k] if near else zero
                        for q in range(COMP):
                            block, cell = (diag, here) if near else (inner, beyond)
                            total = total + block[t, q, :, span] * cell[q][k]
                        pack.append(weight[t] * total)
            pack += weight
            tile = jnp.where(lane == J_ID, own, 0.0)
            for i, v in enumerate(pack):
                tile = jnp.where(lane == i, pltpu.roll(v, (i - (LANES - 1) * side) % LANES, 1), tile)
            half_load(pe).wait()
            end_cells(side)
            for k in range(NPAR):
                jbuf[z, me, 8 * k : 8 * k + 8] = comp[side, k]
            for m in range(1, 4):
                tile = jnp.where(quarter == m, pltpu.roll(tile, J_SPAN * m, 1), tile)
            for m in range(2):
                jbuf[z, me, 16 + m : 17 + m] = jnp.sum(tile[4 * m : 4 * m + 4], axis=0, keepdims=True)
            j_own[...] = own

    def n_copy(side):
        return pltpu.make_async_remote_copy(
            src_ref=n_send.at[side],
            dst_ref=n_recv.at[1 - side],
            send_sem=ns_sem.at[side],
            recv_sem=nr_sem.at[1 - side],
            **to(beside[side]),
        )

    def n_arrival(side):
        return pltpu.make_async_remote_copy(
            src_ref=n_send.at[side],
            dst_ref=n_recv.at[side],
            send_sem=ns_sem.at[side],
            recv_sem=nr_sem.at[side],
            **to(beside[side]),
        )

    def slot(plane):
        return jbuf.at[plane, me, pl.ds(0, ROWS)]

    def z_copy(plane, peer):
        return pltpu.make_async_remote_copy(
            src_ref=slot(plane), dst_ref=slot(plane), send_sem=zs_sem, recv_sem=zr_sem.at[plane], **to(peer)
        )

    def went_straight(plane):
        answer = z < 0
        for source, target in DIRECT:
            answer = jnp.logical_or(answer, jnp.logical_and(z == target, plane == source))
        return answer

    def forward(plane, peers=y_peers):
        for peer in peers:
            pltpu.make_async_remote_copy(
                src_ref=slot(plane), dst_ref=slot(plane), send_sem=ys_sem, recv_sem=yr_sem.at[plane], **to(peer)
            ).start()

    def prepare():
        half_load(1 - pe).wait()

        @pl.when(jnp.logical_not(is_end))
        def _():
            half_load(pe).wait()

        for side in (0, 1):

            @pl.when(interior[side])
            def _():
                end_cells(side)
                end_coefficients(side, True)
                source = []
                for t in range(COMP):
                    total = zero
                    for k in range(NPAR):
                        factor = jnp.where(even, coef[side, PE + NPAR * t + k], coef[side, PN + NPAR * t + k])
                        total = total + factor * comp[side, k]
                    source.append(total)
                after = [nxt(v) for v in source]
                for t in range(COMP):
                    total = source[t]
                    for q in range(COMP):
                        total = total + coef[side, DD + COMP * t + q] * source[q]
                        total = total + coef[side, CIN + COMP * t + q] * after[q]
                    src_s[side, t] = source[t]
                    n_send[side, t] = jnp.where(even, source[t], pltpu.roll(coef[side, WT + t] * total, 1, 1))
                n_send[side, COMP] = lane_pack(
                    [coef[side, COUT + i] for i in range(COMP * COMP)] + [coef[side, WT + t] for t in range(COMP)]
                )

        for side, chosen in ((0, is_first), (1, is_last)):

            @pl.when(chosen)
            def _():
                end_coefficients(side, False)

    def piece():
        def up(v):
            return jnp.where(lane2 == CELLS - 1, 0.0, pltpu.roll(v, CELLS - 1, 1))

        def down(v):
            return jnp.where(lane2 == 0, 0.0, pltpu.roll(v, 1, 1))

        p_here = [[par[t, k] for k in range(NPAR)] for t in range(COMP)]
        p_up = [[up(v) for v in vs] for vs in p_here]
        p_down = [[down(v) for v in vs] for vs in p_here]

        def product(blocks, cells, start):
            rows = []
            for t in range(COMP):
                row = []
                for k in range(NPAR):
                    total = start[t][k] if start is not None else None
                    for q in range(COMP):
                        term = blocks[t, q] * cells[q][k]
                        total = term if total is None else total + term
                    row.append(total)
                rows.append(row)
            return rows

        b0 = product(diag, p_here, p_here)
        bm = product(left, p_down, None)
        bp = product(right, p_up, None)
        weight = [wt[t] for t in range(COMP)]
        u0 = [[weight[t] * v for v in b0[t]] for t in range(COMP)]
        um = [[weight[t] * v for v in bm[t]] for t in range(COMP)]
        upl = [[weight[t] * v for v in bp[t]] for t in range(COMP)]

        def inner_sum(a, b, k, q):
            total = a[0][k] * b[0][q]
            for t in range(1, COMP):
                total = total + a[t][k] * b[t][q]
            return total

        for k in range(NPAR):
            for q in range(NPAR):
                i = NPAR * k + q
                if k <= q:
                    centre = inner_sum(b0, u0, k, q) + down(inner_sum(bp, upl, k, q)) + up(inner_sum(bm, um, k, q))
                    band[8 + i] = centre
                    if k != q:
                        band[8 + NPAR * q + k] = centre
                one = inner_sum(b0, upl, k, q) + up(inner_sum(bm, u0, k, q))
                two = up(inner_sum(bm, upl, k, q))
                band[12 + i] = one
                band[16 + i] = two
                band[4 + NPAR * q + k] = down(one)
                band[NPAR * q + k] = down(down(two))

        def wide_step(r, carry):
            shifted = []
            for k in range(NPAR):
                a = dirs[0, k, r]
                b = dirs[1, k, r]
                per_offset = []
                for off in (-2, -1, 0, 1, 2):
                    if off == 0:
                        per_offset.append((a, b))
                        continue
                    ra = pltpu.roll(a, -off % LANES, 1)
                    rb = pltpu.roll(b, -off % LANES, 1)
                    if off < 0:
                        per_offset.append((ra, jnp.where(lane < -off, ra, rb)))
                    else:
                        per_offset.append((jnp.where(lane >= LANES - off, rb, ra), rb))
                shifted.append(per_offset)
            for half in (0, 1):
                span = slice(half * LANES, half * LANES + LANES)
                for k in range(NPAR):
                    total = None
                    for o in range(5):
                        for q in range(NPAR):
                            term = band[4 * o + NPAR * k + q, :, span] * shifted[q][o][half]
                            total = term if total is None else total + term
                    hess[k, r, :, span] = total
            return carry

        lax.fori_loop(0, COLS, wide_step, 0, unroll=4)

    @pl.when(early)
    def _():
        prepare()
        piece()

    expected = jnp.where(is_end, 1 + len(z_peers) + len(y_peers), 2)
    for source, _ in DIRECT:
        expected = expected + jnp.where(jnp.logical_and(is_end, z == source), len(y_peers), 0)
    pl.semaphore_wait(barrier, expected)

    @pl.when(is_end)
    def _():
        for plane in range(Z_SIZE):

            @pl.when(z != plane)
            def _():
                z_copy(z, (x * Z_SIZE + plane, s)).start()

        for source, target in DIRECT:

            @pl.when(z == source)
            def _():
                forward(z, plane_peers(target))

        forward(z)

    @pl.when(jnp.logical_not(early))
    def _():
        prepare()

    for side in (0, 1):

        @pl.when(interior[side])
        def _():
            n_copy(side).start()

    @pl.when(jnp.logical_not(early))
    def _():
        piece()

    def finish(side):
        change = [coef[side, WT + t] * mean_s[side, t] for t in range(COMP)]
        at_end, at_next = [], []
        for q in range(COMP):
            total = change[q] + mean_a[side, q]
            other = zero
            for t in range(COMP):
                total = total + coef[side, DD + COMP * t + q] * change[t]
                other = other + coef[side, CIN + COMP * t + q] * change[t]
            at_end.append(total)
            at_next.append(other)
        corr = []
        for k in range(NPAR):
            c0, c1 = zero, zero
            for t in range(COMP):
                c0 = c0 + coef[side, PE + NPAR * t + k] * at_end[t]
                c1 = c1 + coef[side, PN + NPAR * t + k] * at_next[t]
            straight = jnp.where(even, c0, pltpu.roll(c1, 1, 1))
            corr.append(swap(straight) if side else straight)
        return corr

    def add_to_piece(side, corr):
        edge = LANES - 2 if side else 0
        here = jnp.logical_and(lane >= edge, lane < edge + 2)
        span = slice(side * LANES, side * LANES + LANES)
        for r in range(COLS):
            for k in range(NPAR):
                moved = pltpu.roll(corr[k], (LANES + edge - 2 * r) % LANES, 1)
                hess[k, r, :, span] = hess[k, r, :, span] + jnp.where(here, moved, 0.0)

    def beside_part():
        for side in (0, 1):

            @pl.when(interior[side])
            def _():
                n_arrival(side).wait_recv()
                theirs = n_recv[side, COMP]
                out_block = [spread(theirs[:, i : i + 1]) for i in range(COMP * COMP)]
                out_weight = [spread(theirs[:, COMP * COMP + t : COMP * COMP + t + 1]) for t in range(COMP)]
                pairs = [n_recv[side, t] for t in range(COMP)]
                adjoint = []
                for t in range(COMP):
                    total, change = zero, zero
                    for q in range(COMP):
                        total = total + out_block[COMP * t + q] * src_s[side, q]
                        change = change + coef[side, COUT + COMP * t + q] * pairs[q]
                    adjoint.append(nxt(pairs[t]) + out_weight[t] * total)
                    mean_s[side, t] = change
                for q in range(COMP):
                    total = zero
                    for t in range(COMP):
                        total = total + out_block[COMP * t + q] * adjoint[t]
                    mean_a[side, q] = total
                add_to_piece(side, finish(side))

    pl.when(early)(beside_part)

    @pl.when(is_end)
    def _():
        for k in reversed(Z_STEPS):
            plane = lax.rem(z + Z_SIZE - k, Z_SIZE)

            @pl.when(jnp.logical_not(went_straight(plane)))
            def _():
                z_copy(plane, z_peers[0]).wait_recv()
                forward(plane)


    pl.when(jnp.logical_not(early))(beside_part)

    @pl.when(is_end)
    def _():
        own = j_own[...]
        rows = 8 * PIPES

        def arrivals(planes, sem):
            span = jbuf.at[planes, pl.ds(0, 7), pl.ds(0, ROWS)]
            return pltpu.make_async_remote_copy(
                src_ref=span, dst_ref=span, send_sem=ys_sem, recv_sem=yr_sem.at[sem], **to(y_peers[0])
            )

        j_sum[...] = jnp.zeros_like(j_sum)
        j_weight[...] = jnp.zeros_like(j_weight)
        degree = zero
        for end in (0, 1):
            for half in (0, 1):
                row = ids[end, :, half * LANES : half * LANES + LANES].astype(F32)
                degree = degree + jnp.where(row == own, 1.0, 0.0)
        share = 1.0 / spread(jnp.sum(degree, axis=1, keepdims=True))

        def add_planes(j, carry):
            pair = [lax.rem(z + Z_SIZE - j, Z_SIZE), lax.rem(z + 1 + j, Z_SIZE)]
            columns, tiles = [], []
            for plane in pair:
                arrivals(plane, plane).wait_recv()

                @pl.when(went_straight(plane))
                def _():
                    z_copy(plane, z_peers[0]).wait_recv()

                halves = [jbuf[plane, :, 8 * k : 8 * k + 8].reshape(rows, LANES) for k in range(NPAR)]
                columns.append(split(jnp.concatenate(halves, axis=1)))
                for q in range(8):
                    packed = jnp.where(
                        iota((PIPES, LANES), 0) < 4, jbuf[plane, q, 16:17], jbuf[plane, q, 17:18]
                    )
                    tile = packed
                    for m in range(1, 4):
                        tile = jnp.where(quarter == m, pltpu.roll(packed, LANES - J_SPAN * m, 1), tile)
                    tiles.append(tile)
            x_parts = [jnp.concatenate([c[i] for c in columns]) for i in range(3)]
            coefs = jnp.concatenate(tiles).T
            same = coefs[J_ID : J_ID + 1] == own[:, 0:1]
            w_parts = [
                jnp.concatenate([jnp.where(same, v[i : i + 1], 0.0) for i in range(J_W)]).astype(BF16)
                for v in split(coefs[:J_SPAN], F32)
            ]
            order = ((0, 0), (0, 1), (1, 0), (0, 2), (2, 0), (1, 1))
            j_sum[...] += jnp.dot(
                jnp.concatenate([w_parts[i] for i, _ in order], axis=1),
                jnp.concatenate([x_parts[i] for _, i in order]),
                preferred_element_type=F32,
            )
            for t in range(COMP):
                j_weight[t] += jnp.where(same, coefs[J_W + t : J_W + t + 1], 0.0)
            return carry

        lax.fori_loop(0, Z_SIZE // 2, add_planes, 0)

        def part(c, k):
            return j_sum[PIPES * c : PIPES * c + PIPES, LANES * k : LANES * k + LANES]

        for t in range(COMP):
            c = NPAR * t
            mean = share * (part(c, 0) + part(c + 1, 1))
            near = part(8 + c, 0) + part(9 + c, 1)
            far = part(16 + c, 0) + part(17 + c, 1)
            weights = spread(jnp.sum(j_weight[t], axis=1, keepdims=True))
            mean_s[pe, t] = 0.5 * mean
            mean_a[pe, t] = 0.5 * share * (near + nxt(far) + 0.5 * weights * mean)
        for side, chosen in ((0, is_first), (1, is_last)):

            @pl.when(chosen)
            def _():
                for k, v in enumerate(finish(side)):
                    last[k] = v

        for plane in range(Z_SIZE):
            sent = z < 0
            for source, target in DIRECT:
                if source == plane:
                    sent = jnp.logical_or(sent, z == target)

            @pl.when(jnp.logical_not(sent))
            def _():
                arrivals(plane, plane).wait_send()

        for source, target in DIRECT:

            @pl.when(z == source)
            def _():
                arrivals(target, target).wait_send()

        span = jbuf.at[0, pl.ds(0, 7), pl.ds(0, ROWS)]
        pltpu.make_async_remote_copy(
            src_ref=span, dst_ref=span, send_sem=zs_sem, recv_sem=yr_sem.at[0], **to(z_peers[0])
        ).wait_send()

    for side in (0, 1):

        @pl.when(interior[side])
        def _():
            n_copy(side).wait_send()


def write_kernel(hess, last, out, piece, sem):
    s = lax.axis_index("sub")
    lane = iota((PIPES, LANES), 1)

    def write(side, k, source):
        span = pl.ds(side * LANES, LANES)
        return pltpu.make_async_copy(source, out.at[k, :, :, span], sem.at[side, k])

    for side in (0, 1):

        @pl.when(s != 7 * side)
        def _():
            for k in range(NPAR):
                write(side, k, hess.at[k, :, :, pl.ds(side * LANES, LANES)]).start()

    for side in (0, 1):

        @pl.when(s == 7 * side)
        def _():
            edge = LANES - 2 if side else 0
            here = jnp.logical_and(lane >= edge, lane < edge + 2)
            for k in range(NPAR):
                corr = last[k]
                for r in range(COLS):
                    moved = pltpu.roll(corr, (LANES + edge - 2 * r) % LANES, 1)
                    piece[k, r] = hess[k, r, :, side * LANES : side * LANES + LANES] + jnp.where(here, moved, 0.0)
                write(side, k, piece.at[k]).start()

    for side in (0, 1):
        for k in range(NPAR):
            write(side, k, piece.at[k]).wait()


def on_device(directions, diag_blocks, left_blocks, right_blocks, param_blocks, obs_weight, end_junction):
    args = (directions, diag_blocks, left_blocks, right_blocks, param_blocks, obs_weight, jnp.swapaxes(end_junction, 1, 2))
    args = tuple(pltpu.with_memory_space_constraint(a, pltpu.HBM) for a in args)
    dma = pltpu.SemaphoreType.DMA

    def tiles(*counts):
        return pltpu.VMEM(counts + (PIPES, LANES), F32)

    hess, last = pl.pallas_call(
        kernel,
        out_shape=(pltpu.VMEM(directions.shape, F32), tiles(NPAR)),
        in_specs=[pl.BlockSpec(memory_space=pl.ANY)] * len(args),
        out_specs=[pl.BlockSpec(memory_space=pltpu.VMEM)] * 2,
        scratch_shapes=[tiles(2, NPAR, COLS)]
        + [pltpu.VMEM(a.shape, a.dtype) for a in args[1:]]
        + [
            pltpu.VMEM((5 * NPAR * NPAR, PIPES, CELLS), F32),
            tiles(2, N_COEF),
            tiles(2, NPAR),
            tiles(2, COMP),
            tiles(2, COMP + 1),
            tiles(2, COMP + 1),
            pltpu.VMEM((Z_SIZE, 8, 24, LANES), F32),
            pltpu.VMEM((PIPES * J_W, 2 * LANES), F32),
            tiles(COMP),
            tiles(),
            tiles(2, COMP),
            tiles(2, COMP),
            dma((2,)),
            dma((6,)),
            dma((2,)),
            dma((2,)),
            dma,
            dma((8,)),
            dma,
            dma((8,)),
        ],
        compiler_params=pltpu.CompilerParams(
            collective_id=3, has_side_effects=True, vmem_limit_bytes=56 * 1024 * 1024
        ),
    )(*args)
    return pl.pallas_call(
        write_kernel,
        out_shape=jax.ShapeDtypeStruct(directions.shape, F32),
        in_specs=[pl.BlockSpec(memory_space=pltpu.VMEM)] * 2,
        out_specs=pl.BlockSpec(memory_space=pl.ANY),
        scratch_shapes=[tiles(NPAR, COLS), dma((2, NPAR))],
    )(*(pltpu.with_memory_space_constraint(v, pltpu.VMEM) for v in (hess, last)))


def solution(mesh):
    return jax.shard_map(
        on_device,
        mesh=mesh,
        in_specs=(
            P(None, None, "region", "sub"),
            P(None, None, "region", "sub"),
            P(None, None, "region", "sub"),
            P(None, None, "region", "sub"),
            P(None, None, "region", "sub"),
            P(None, "region", "sub"),
            P(),
        ),
        out_specs=P(None, None, "region", "sub"),
        check_vma=False,
    )
```
